32 devices in a mesh: cube: 4 (over z), row: 4 (over y, core), col: 2 (over x).
Axes of the slice: x: 2, y: 2, z: 4, core: 2. Of those that a mesh axis runs over, the one named last changes fastest.
Arguments:
- diag_block: float32 [4, 256, 256], P('cube', ('row', 'col'))
- pivot_order: int32 [4, 256], P('cube'), may hold values from 0 to 255, as said below
- lower_in: bfloat16 [4, 4096, 256], P('cube', 'row', 'col'), may hold values from -0.14941406 to 0.14941406
- upper_in: bfloat16 [4, 256, 30720], P('cube', 'row', 'col'), may hold values from -6 to 6
- trailing: bfloat16 [4, 4096, 30720], P('cube', 'row', 'col'), may hold values from -6 to 6
- block_mask: int32 [4, 32, 4], P('cube', 'row', 'col'), may hold values 0 or 1
- row_map: int32 [4, 4096], P('cube', 'row'), may hold values from 0 to 1023, as said below
Outputs:
- merged: bfloat16 [4, 4096, 15360], P('cube', 'row', 'col')
The draws below stay inside these ranges and needn't reach their ends.
Inputs may be any that keep to these rules, and one draw needn't show every extreme that they name: `pivot_order`: each front's row is a permutation of 0 to 255. `row_map`: in each aligned block of 1024 rows of a front the entries are a permutation of 0 to 1023.
All inputs are finite; a program needn't handle non-finite values. No bound on the sum of `block_mask` on one device may be relied on, other than what follows from the above.
Results may differ from the reference program's by a relative error of at most 0.0056.
Values may be sent and summed in bfloat16 or wider, within the bound.
No kernel may reach another device: no remote copies, remote signals or barrier semaphores. Data moves between devices by JAX's collectives and lax.ppermute only.
A program may use at most 320 MiB of HBM per device.

```python
import jax
import jax.numpy as jnp
from jax import lax

NB = 256
NF = 30720
M_DEV = 1024
BR = 128
FRONTS = 4
M = 4096
N_COL = 2


def pivot_helper(key):
    keys = jax.random.split(jax.random.fold_in(key, 11), FRONTS)
    return jax.vmap(lambda single: jax.random.permutation(single, NB))(keys).astype(jnp.int32)


def draw_pivot_order(key, part):
    return pivot_helper(key)


def draw_diag_block(key, part):
    order = pivot_helper(key)
    lower_key = jax.random.fold_in(key, 23)
    upper_key = jax.random.fold_in(key, 31)
    diag_key = jax.random.fold_in(key, 37)
    shape = (FRONTS, NB, NB)
    lower_ints = jax.random.randint(jax.random.fold_in(lower_key, 1), shape, -4, 5, dtype=jnp.int32) + jax.random.randint(jax.random.fold_in(lower_key, 2), shape, -4, 5, dtype=jnp.int32)
    upper_ints = jax.random.randint(jax.random.fold_in(upper_key, 1), shape, -4, 5, dtype=jnp.int32) + jax.random.randint(jax.random.fold_in(upper_key, 2), shape, -4, 5, dtype=jnp.int32)
    diag_ints = jax.random.randint(diag_key, (FRONTS, NB), 24, 175, dtype=jnp.int32)
    rows = jnp.arange(NB, dtype=jnp.int32)[:, None]
    cols = jnp.arange(NB, dtype=jnp.int32)[None, :]
    below = (rows > cols).astype(jnp.int32)
    above = (rows < cols).astype(jnp.int32)
    ident = (rows == cols).astype(jnp.int32)
    unit_lower = lower_ints * below[None] + 64 * ident[None]
    upper_tri = upper_ints * above[None] + diag_ints[:, :, None] * ident[None]
    product = jnp.matmul(unit_lower, upper_tri)
    base = product.astype(jnp.float32) / 4096.0
    return jax.vmap(lambda block_rows, perm: jnp.zeros((NB, NB), jnp.float32).at[perm].set(block_rows))(base, order)


def draw_row_map(key, part):
    count = FRONTS * (M // M_DEV)
    keys = jax.random.split(jax.random.fold_in(key, 5), count)
    perms = jax.vmap(lambda single: jax.random.permutation(single, M_DEV))(keys)
    return perms.reshape(FRONTS, M).astype(jnp.int32)


def place_ends(entries, stream_key, least, top_value):
    longest = entries.shape.index(max(entries.shape))
    spots = []
    for shift in (0, 1):
        where = [jax.random.randint(jax.random.fold_in(stream_key, axis), (), 0, length) for axis, length in enumerate(entries.shape)]
        where[longest] = (where[longest] + shift) % entries.shape[longest]
        spots.append(tuple(where))
    return entries.at[spots[0]].set(least).at[spots[1]].set(top_value)


def levels(own_key, dims, cuts, low, high):
    factor_of, own = 1.0, jax.random.fold_in(own_key, 6)
    for position, parts in cuts:
        steps = jnp.exp(jax.random.uniform(jax.random.fold_in(own, position), (parts,), jnp.float32, low / len(cuts), high / len(cuts)))
        factor_of = factor_of * jnp.repeat(steps, dims[position] // parts).reshape([-1 if axis == position else 1 for axis in range(len(dims))])
    return factor_of


def gaussian(rng, dims, scale, limit, cuts=(), held_as=jnp.bfloat16):
    result = jax.random.normal(rng, dims, jnp.float32) * scale
    if len(cuts) > 0:
        result = levels(rng, dims, cuts, -0.22, 0.18) * result
    return jnp.clip(result, min=-limit, max=limit).astype(held_as)


def setup_inputs(seed: int = 0) -> dict:
    splits = jax.random.split(jax.random.key(seed), 8)
    return {
        "diag_block": draw_diag_block(jax.random.fold_in(splits[7], 71), 0),
        "pivot_order": draw_pivot_order(jax.random.fold_in(splits[7], 71), 0),
        "lower_in": gaussian(splits[2], (FRONTS, M, NB), 0.025, 0.14941406, ((0, 4), (1, 4), (2, 2))),
        "upper_in": gaussian(splits[3], (FRONTS, NB, NF), 1.0, 6.0, ((0, 4), (1, 4), (2, 2))),
        "trailing": gaussian(splits[4], (FRONTS, M, NF), 1.0, 6.0, ((0, 4), (1, 4), (2, 2))),
        "block_mask": place_ends((jax.random.randint(splits[5], (FRONTS, M // BR, 2 * N_COL), 0, 4) < 3).astype(jnp.int32), jax.random.fold_in(splits[5], 1), 0, 1),
        "row_map": draw_row_map(jax.random.fold_in(splits[7], 71), 0),
    }


def exact_product(left, right):
    return jnp.dot(left, right, precision=lax.Precision.HIGHEST, preferred_element_type=left.dtype)


def small_inverses(block):
    size = block.shape[0]
    work = block
    for step in range(size - 1):
        column = work[step + 1:, step] / work[step, step]
        work = work.at[step + 1:, step + 1:].add(-column[:, None] * work[step, step + 1:][None, :])
        work = work.at[step + 1:, step].set(column)
    identity = jnp.eye(size, dtype=block.dtype)
    lower = jnp.tril(work, -1) + identity
    upper = jnp.triu(work)
    lower_rows = []
    for step in range(size):
        fresh = identity[step]
        for inner in range(step):
            fresh = fresh - lower[step, inner] * lower_rows[inner]
        lower_rows.append(fresh)
    upper_rows = [None] * size
    for step in range(size - 1, -1, -1):
        fresh = identity[step]
        for inner in range(step + 1, size):
            fresh = fresh - upper[step, inner] * upper_rows[inner]
        upper_rows[step] = fresh / upper[step, step]
    return jnp.stack(lower_rows), jnp.stack(upper_rows)


def block_inverses(block):
    size = block.shape[0]
    if size <= 8:
        return small_inverses(block)
    half = size // 2
    lower_one, upper_one = block_inverses(block[:half, :half])
    lower_side = exact_product(block[half:, :half], upper_one)
    upper_side = exact_product(lower_one, block[:half, half:])
    schur = block[half:, half:] - exact_product(lower_side, upper_side)
    lower_two, upper_two = block_inverses(schur)
    zero = jnp.zeros((half, half), block.dtype)
    corner_lower = -exact_product(lower_two, exact_product(lower_side, lower_one))
    corner_upper = -exact_product(upper_one, exact_product(upper_side, upper_two))
    lower_inv = jnp.concatenate([jnp.concatenate([lower_one, zero], axis=1), jnp.concatenate([corner_lower, lower_two], axis=1)], axis=0)
    upper_inv = jnp.concatenate([jnp.concatenate([upper_one, corner_upper], axis=1), jnp.concatenate([zero, upper_two], axis=1)], axis=0)
    return lower_inv, upper_inv


def front_update(diag, order, below_panel, right_panel, block, mask):
    lower_inv, upper_inv = block_inverses(jnp.take(diag, order, axis=0))
    lower_panel = jnp.dot(below_panel.astype(jnp.float32), upper_inv, precision=lax.Precision.HIGHEST, preferred_element_type=jnp.float32).astype(jnp.bfloat16)
    upper_panel = jnp.dot(lower_inv, jnp.take(right_panel, order, axis=0).astype(jnp.float32), precision=lax.Precision.HIGHEST, preferred_element_type=jnp.float32).astype(jnp.bfloat16)
    product = jnp.dot(lower_panel, upper_panel, preferred_element_type=jnp.float32)
    blocks, tiles = mask.shape
    masked = (product.reshape(blocks, -1, tiles, product.shape[1] // tiles) * mask.astype(jnp.float32)[:, None, :, None]).reshape(product.shape)
    return (block.astype(jnp.float32) - masked).astype(jnp.bfloat16)


def extend_add(mine, other, mapping, side):
    width = NF // (2 * N_COL)
    kept = mine.reshape(M, N_COL, 2, width)[:, :, side, :]
    starts = (jnp.arange(M, dtype=jnp.int32) // M_DEV) * M_DEV
    source = (starts + mapping).astype(jnp.int32)
    taken = jnp.take(other.reshape(M, N_COL, 2, width), source, axis=0)[:, :, side, :]
    return (kept.astype(jnp.float32) + taken.astype(jnp.float32)).astype(jnp.bfloat16).reshape(M, NF // 2)


def reference(diag_block, pivot_order, lower_in, upper_in, trailing, block_mask, row_map):
    pairs = FRONTS // 2

    def per_pair(items):
        diag, order, below_panel, right_panel, block, mask, mapping = items
        first = front_update(diag[0], order[0], below_panel[0], right_panel[0], block[0], mask[0])
        second = front_update(diag[1], order[1], below_panel[1], right_panel[1], block[1], mask[1])
        return (extend_add(first, second, mapping[0], 0), extend_add(second, first, mapping[1], 1))

    inputs = (diag_block, pivot_order, lower_in, upper_in, trailing, block_mask, row_map)
    stacked = tuple(item.reshape((pairs, 2) + item.shape[1:]) for item in inputs)
    even_out, odd_out = lax.map(per_pair, stacked)
    return jnp.stack([even_out, odd_out], axis=1).reshape(FRONTS, M, NF // 2)
```

```python
import functools

import jax
import jax.numpy as jnp
from jax import lax
from jax.experimental import pallas as pl
from jax.experimental.pallas import tpu as pltpu
from jax.sharding import PartitionSpec as P

CHUNKS = 15
ROW_STEPS = 4
HIGH = lax.Precision.HIGHEST
VMEM_LIMIT = 48 * 1024 * 1024


def partner(block, axis, bits):
    count = lax.axis_size(axis)
    return lax.ppermute(block, axis, [(i, i ^ bits) for i in range(count)])


def exact(left, right):
    return jnp.dot(left, right, precision=HIGH, preferred_element_type=jnp.float32)


def fast(left, right):
    return jnp.dot(left, right, preferred_element_type=jnp.float32)


def split(value):
    high = value.astype(jnp.bfloat16)
    return high, (value - high.astype(jnp.float32)).astype(jnp.bfloat16)


def eliminate(block):
    size = block.shape[0]
    row = lax.broadcasted_iota(jnp.int32, (size, size), 0)
    lane = lax.broadcasted_iota(jnp.int32, (size, size), 1)

    def eight(turn, work):
        left = size - 8 * turn
        for step in range(8):
            column = work[:, step : step + 1]
            pivot_row = work[step : step + 1, :]
            inverse = 1.0 / work[step : step + 1, step : step + 1]
            scaled = pivot_row * inverse
            lane_one = lane[:1]
            at = lane_one == step
            passed = (lane_one < step) | (lane_one >= left)
            for_later = jnp.where(at, inverse, scaled)
            for_passed = jnp.where(passed | at, 0.0, scaled)
            row_passed = (row < step) | (row >= left)
            base = jnp.where((lane == step) & jnp.logical_not(row_passed), 0.0, work)
            fresh = base - column * jnp.where(row_passed, for_passed, for_later)
            own = jnp.where(at, inverse, jnp.where(passed, pivot_row, -scaled))
            work = jnp.where(row == step, own, fresh)
        work = jnp.concatenate([work[8:], work[:8]], axis=0)
        return pltpu.roll(work, size - 8, 1)

    return lax.fori_loop(0, size // 8, eight, block)


def inverses(block):
    size = block.shape[0]
    work = eliminate(block)
    row = lax.broadcasted_iota(jnp.int32, (size, size), 0)
    lane = lax.broadcasted_iota(jnp.int32, (size, size), 1)
    diagonal = jnp.sum(jnp.where(row == lane, work, 0.0), axis=0, keepdims=True)
    lower = jnp.where(row > lane, work, jnp.where(row == lane, 1.0, 0.0))
    upper = jnp.where(row < lane, work * diagonal, jnp.where(row == lane, work, 0.0))
    return lower, upper


def factor_kernel(block, order_of_diag, order_of_upper, order_of_lower, panel, mask, hi, lo, sent, kept):
    size = block.shape[0]
    half = size // 2
    lane = lax.broadcasted_iota(jnp.int32, (size, size), 1)

    def chosen(order):
        return jnp.where(order[...] == lane, 1.0, 0.0)

    pivoted = exact(chosen(order_of_diag), block[...])
    lower_one, upper_one = inverses(pivoted[:half, :half])
    lower_side = exact(pivoted[half:, :half], upper_one)
    upper_side = exact(lower_one, pivoted[:half, half:])
    schur = pivoted[half:, half:] - exact(lower_side, upper_side)
    lower_two, upper_two = inverses(schur)
    zero = jnp.zeros((half, half), jnp.float32)
    corner_lower = -exact(lower_two, exact(lower_side, lower_one))
    corner_upper = -exact(upper_one, exact(upper_side, upper_two))
    lower_inv = jnp.concatenate(
        [jnp.concatenate([lower_one, zero], 1), jnp.concatenate([corner_lower, lower_two], 1)], 0
    )
    upper_inv = jnp.concatenate(
        [jnp.concatenate([upper_one, corner_upper], 1), jnp.concatenate([zero, upper_two], 1)], 0
    )
    hi[...], lo[...] = split(exact(lower_inv, chosen(order_of_upper)))
    upper_hi, upper_lo = split(exact(chosen(order_of_lower), upper_inv))
    for start in range(0, panel.shape[0], size):
        rows = slice(start, start + size)
        part = panel[rows, :]
        result = fast(part, upper_hi) + fast(part, upper_lo)
        result = result.astype(jnp.bfloat16).astype(jnp.float32)
        sent[rows, :] = (result * mask[rows, 0:1]).astype(jnp.bfloat16)
        kept[rows, :] = (result * mask[rows, 1:2]).astype(jnp.bfloat16)


def factor(block, orders, panel, mask):
    size = block.shape[0]
    rows = panel.shape[0]
    half_type = jnp.bfloat16
    return pl.pallas_call(
        factor_kernel,
        out_shape=(
            jax.ShapeDtypeStruct((size, size), half_type),
            jax.ShapeDtypeStruct((size, size), half_type),
            jax.ShapeDtypeStruct((rows, size), half_type),
            jax.ShapeDtypeStruct((rows, size), half_type),
        ),
        compiler_params=pltpu.CompilerParams(vmem_limit_bytes=VMEM_LIMIT),
        cost_estimate=pl.CostEstimate(flops=30_000_000_000, bytes_accessed=3_000_000, transcendentals=0),
        name="factor",
    )(block, *orders, panel, mask)


def panel_tile(hi, lo, pieces):
    columns = jnp.concatenate([piece[...] for piece in pieces], axis=0)
    return (fast(hi[...], columns) + fast(lo[...], columns)).astype(jnp.bfloat16)


def send_kernel(place, hi, lo, left, trailing, *rest):
    *pieces, out, right = rest

    @pl.when(pl.program_id(0) == 0)
    def _():
        right[...] = panel_tile(hi, lo, pieces)

    out[...] = (trailing[...].astype(jnp.float32) - fast(left[...], right[...])).astype(jnp.bfloat16)


def merge_kernel(place, hi, lo, left, trailing, chosen, received, *rest):
    *pieces, out, right = rest

    @pl.when(pl.program_id(0) == 0)
    def _():
        right[...] = panel_tile(hi, lo, pieces)

    own = (trailing[...].astype(jnp.float32) - fast(left[...], right[...])).astype(jnp.bfloat16)
    out[...] = (own.astype(jnp.float32) + fast(chosen[...], received[...])).astype(jnp.bfloat16)


def merge_kernel_into(place, hi, lo, left, trailing, chosen, received, *rest):
    *pieces, _, out, right = rest
    merge_kernel(place, hi, lo, left, trailing, chosen, received, *pieces, out, right)


def specs_for(hi, left, width, steps, half_blocks, chunk, pieces, starts):
    size = hi.shape[0]
    rows = left.shape[0] // steps
    whole = pl.BlockSpec((size, size), lambda i, place: (0, 0))
    specs = [
        whole,
        whole,
        pl.BlockSpec((rows, size), lambda i, place: (i, 0)),
        pl.BlockSpec((rows, width), lambda i, place: (i, place[0] * half_blocks + chunk)),
    ]
    piece_specs = []
    for number, (piece, start) in enumerate(zip(pieces, starts)):
        depth = piece.shape[0]
        if number == 0:
            piece_specs.append(pl.BlockSpec((depth, width), lambda i, place: (0, place[0] * half_blocks + chunk)))
        else:
            piece_specs.append(pl.BlockSpec((depth, width), lambda i, place, at=chunk - start: (0, at)))
    return specs, piece_specs


def send_chunk(place, hi, lo, left, trailing, pieces, starts, width, chunk):
    rows, columns = trailing.shape
    half_blocks = columns // 2 // width
    specs, piece_specs = specs_for(hi, left, width, ROW_STEPS, half_blocks, chunk, pieces, starts)
    return pl.pallas_call(
        send_kernel,
        grid_spec=pltpu.PrefetchScalarGridSpec(
            num_scalar_prefetch=1,
            grid=(ROW_STEPS,),
            in_specs=specs + piece_specs,
            out_specs=pl.BlockSpec((rows // ROW_STEPS, width), lambda i, place: (i, 0)),
            scratch_shapes=[pltpu.VMEM((hi.shape[0], width), jnp.bfloat16)],
        ),
        out_shape=jax.ShapeDtypeStruct((rows, width), jnp.bfloat16),
        compiler_params=pltpu.CompilerParams(vmem_limit_bytes=VMEM_LIMIT),
        cost_estimate=pl.CostEstimate(flops=2 * rows * 256 * width, bytes_accessed=5 * rows * width, transcendentals=0),
        name="send_part",
    )(place, hi, lo, left, trailing, *pieces)


def merge_chunk(place, hi, lo, left, trailing, chosen, received, pieces, starts, width, chunk, merged):
    rows, columns = trailing.shape
    half_blocks = columns // 2 // width
    step_rows = rows // ROW_STEPS
    specs, piece_specs = specs_for(hi, left, width, ROW_STEPS, half_blocks, chunk, pieces, starts)
    specs += [
        pl.BlockSpec((step_rows, rows), lambda i, place: (i, 0)),
        pl.BlockSpec((rows, width), lambda i, place: (0, 0)),
    ] + piece_specs
    operands = [place, hi, lo, left, trailing, chosen, received, *pieces]
    aliases = {}
    body = merge_kernel
    if merged is not None:
        aliases = {len(operands): 0}
        operands.append(merged)
        specs.append(pl.BlockSpec(memory_space=pl.ANY))
        body = merge_kernel_into
    return pl.pallas_call(
        body,
        grid_spec=pltpu.PrefetchScalarGridSpec(
            num_scalar_prefetch=1,
            grid=(ROW_STEPS,),
            in_specs=specs,
            out_specs=pl.BlockSpec((step_rows, width), lambda i, place: (i, chunk)),
            scratch_shapes=[pltpu.VMEM((hi.shape[0], width), jnp.bfloat16)],
        ),
        out_shape=jax.ShapeDtypeStruct((rows, columns // 2), jnp.bfloat16),
        input_output_aliases=aliases,
        compiler_params=pltpu.CompilerParams(vmem_limit_bytes=VMEM_LIMIT),
        cost_estimate=pl.CostEstimate(flops=2 * rows * (rows + 256) * width, bytes_accessed=8 * rows * width, transcendentals=0),
        name="merge_part",
    )(*operands)


def doubled(block, axis, dimension):
    bits = 1
    while bits < lax.axis_size(axis):
        block = jnp.concatenate([block, partner(block, axis, bits)], axis=dimension)
        bits *= 2
    return block


def relative(index, part, me):
    return ((index // part) ^ me) * part + index % part


def local(diag_block, pivot_order, lower_in, upper_in, trailing, block_mask, row_map):
    diag_block, lower_in, upper_in, trailing = diag_block[0], lower_in[0], upper_in[0], trailing[0]
    size = diag_block.shape[1]
    rows, columns = trailing.shape
    half = columns // 2
    width = half // CHUNKS
    group = lax.axis_index(("row", "col"))
    row, col = lax.axis_index("row"), lax.axis_index("col")
    parity = lax.axis_index("cube") % 2
    sent_place = (1 - parity).astype(jnp.int32).reshape(1)
    kept_place = parity.astype(jnp.int32).reshape(1)

    whole_block = doubled(diag_block, ("row", "col"), 0)
    panel = doubled(lower_in, "col", 1)
    order = pivot_order[0][:, None]
    orders = (
        relative(order, diag_block.shape[0], group),
        relative(order, upper_in.shape[0], row),
        relative(jnp.arange(size, dtype=jnp.int32)[:, None], lower_in.shape[1], col),
    )
    flags = jnp.repeat(block_mask[0].astype(jnp.float32), rows // block_mask.shape[1], axis=0)
    flags = jnp.where(parity == 0, flags[:, ::-1], flags)
    chosen = (row_map[0][:, None] == jnp.arange(rows, dtype=jnp.int32)[None, :]).astype(jnp.bfloat16)

    def gathered(place, first, last):
        own = lax.dynamic_slice_in_dim(upper_in, place * half + first * width, (last - first) * width, 1)
        return [partner(own, "row", bits) for bits in range(1, lax.axis_size("row"))]

    cuts = (0, 2, 7, CHUNKS)
    sent_groups = [(a, b, gathered(1 - parity, a, b)) for a, b in zip(cuts, cuts[1:])]
    kept_groups = [(0, CHUNKS, gathered(parity, 0, CHUNKS))]

    def pieces_of(groups, chunk):
        for first, last, arrays in groups:
            if first <= chunk < last:
                return [upper_in, *arrays], [0] + [first] * len(arrays)

    hi, lo, sent_left, kept_left = factor(whole_block, orders, panel, flags)

    received = []
    for chunk in range(CHUNKS):
        pieces, starts = pieces_of(sent_groups, chunk)
        outgoing = send_chunk(sent_place, hi, lo, sent_left, trailing, pieces, starts, width, chunk)
        received.append(partner(outgoing, "cube", 1))
    merged = None
    for chunk in range(CHUNKS):
        pieces, starts = pieces_of(kept_groups, chunk)
        merged = merge_chunk(
            kept_place, hi, lo, kept_left, trailing, chosen, received[chunk], pieces, starts, width, chunk, merged
        )
    return merged[None]


def solution(mesh):
    return jax.shard_map(
        local,
        mesh=mesh,
        in_specs=(
            P("cube", ("row", "col"), None),
            P("cube", None),
            P("cube", "row", "col"),
            P("cube", "row", "col"),
            P("cube", "row", "col"),
            P("cube", "row", "col"),
            P("cube", "row"),
        ),
        out_specs=P("cube", "row", "col"),
        check_vma=False,
    )
```

```python
import functools

import jax
import jax.numpy as jnp
from jax import lax
from jax.experimental import pallas as pl
from jax.experimental.pallas import tpu as pltpu
from jax.sharding import PartitionSpec as P

CHUNKS = 15
RAW = 2
EARLY = 2
AHEAD = 3
BEHIND = 6
ROW_STEPS = 4
HIGH = lax.Precision.HIGHEST
VMEM_LIMIT = 48 * 1024 * 1024


def partner(block, axis, bits):
    count = lax.axis_size(axis)
    return lax.ppermute(block, axis, [(i, i ^ bits) for i in range(count)])


def exact(left, right):
    return jnp.dot(left, right, precision=HIGH, preferred_element_type=jnp.float32)


def fast(left, right):
    return jnp.dot(left, right, preferred_element_type=jnp.float32)


def split(value):
    high = value.astype(jnp.bfloat16)
    return high, (value - high.astype(jnp.float32)).astype(jnp.bfloat16)


def eliminate(block):
    size = block.shape[0]
    row = lax.broadcasted_iota(jnp.int32, (size, size), 0)
    lane = lax.broadcasted_iota(jnp.int32, (size, size), 1)

    def eight(turn, work):
        left = size - 8 * turn
        for step in range(8):
            column = work[:, step : step + 1]
            pivot_row = work[step : step + 1, :]
            inverse = 1.0 / work[step : step + 1, step : step + 1]
            scaled = pivot_row * inverse
            lane_one = lane[:1]
            at = lane_one == step
            passed = (lane_one < step) | (lane_one >= left)
            for_later = jnp.where(at, inverse, scaled)
            for_passed = jnp.where(passed | at, 0.0, scaled)
            row_passed = (row < step) | (row >= left)
            base = jnp.where((lane == step) & jnp.logical_not(row_passed), 0.0, work)
            fresh = base - column * jnp.where(row_passed, for_passed, for_later)
            own = jnp.where(at, inverse, jnp.where(passed, pivot_row, -scaled))
            work = jnp.where(row == step, own, fresh)
        work = jnp.concatenate([work[8:], work[:8]], axis=0)
        return pltpu.roll(work, size - 8, 1)

    return lax.fori_loop(0, size // 8, eight, block)


def inverses(block):
    size = block.shape[0]
    work = eliminate(block)
    row = lax.broadcasted_iota(jnp.int32, (size, size), 0)
    lane = lax.broadcasted_iota(jnp.int32, (size, size), 1)
    diagonal = jnp.sum(jnp.where(row == lane, work, 0.0), axis=0, keepdims=True)
    lower = jnp.where(row > lane, work, jnp.where(row == lane, 1.0, 0.0))
    upper = jnp.where(row < lane, work * diagonal, jnp.where(row == lane, work, 0.0))
    return lower, upper


def factor_kernel(block, order_of_diag, order_of_upper, order_of_lower, panel, mask, hi, lo, plain, sent, kept):
    size = block.shape[0]
    half = size // 2
    lane = lax.broadcasted_iota(jnp.int32, (size, size), 1)

    def chosen(order):
        return jnp.where(order[...] == lane, 1.0, 0.0)

    pivoted = exact(chosen(order_of_diag), block[...])
    lower_one, upper_one = inverses(pivoted[:half, :half])
    lower_side = exact(pivoted[half:, :half], upper_one)
    upper_side = exact(lower_one, pivoted[:half, half:])
    schur = pivoted[half:, half:] - exact(lower_side, upper_side)
    lower_two, upper_two = inverses(schur)
    zero = jnp.zeros((half, half), jnp.float32)
    corner_lower = -exact(lower_two, exact(lower_side, lower_one))
    corner_upper = -exact(upper_one, exact(upper_side, upper_two))
    lower_inv = jnp.concatenate(
        [jnp.concatenate([lower_one, zero], 1), jnp.concatenate([corner_lower, lower_two], 1)], 0
    )
    upper_inv = jnp.concatenate(
        [jnp.concatenate([upper_one, corner_upper], 1), jnp.concatenate([zero, upper_two], 1)], 0
    )
    hi[...], lo[...] = split(exact(lower_inv, chosen(order_of_upper)))
    row = lax.broadcasted_iota(jnp.int32, (size, size), 0)
    in_order = jnp.where(order_of_lower[...] == row, 1.0, 0.0)
    upper_hi, upper_lo = split(exact(in_order, upper_inv))
    for start in range(0, panel.shape[0], size):
        rows = slice(start, start + size)
        part = panel[rows, :]
        result = fast(part, upper_hi) + fast(part, upper_lo)
        plain[rows, :] = result.astype(jnp.bfloat16)
        result = result.astype(jnp.bfloat16).astype(jnp.float32)
        sent[rows, :] = (result * mask[rows, 0:1]).astype(jnp.bfloat16)
        kept[rows, :] = (result * mask[rows, 1:2]).astype(jnp.bfloat16)


def factor(block, orders, panel, mask):
    size = block.shape[0]
    rows = panel.shape[0]
    half_type = jnp.bfloat16
    return pl.pallas_call(
        factor_kernel,
        out_shape=(
            jax.ShapeDtypeStruct((size, size), half_type),
            jax.ShapeDtypeStruct((size, size), half_type),
            jax.ShapeDtypeStruct((rows, size), half_type),
            jax.ShapeDtypeStruct((rows, size), half_type),
            jax.ShapeDtypeStruct((rows, size), half_type),
        ),
        compiler_params=pltpu.CompilerParams(vmem_limit_bytes=VMEM_LIMIT),
        cost_estimate=pl.CostEstimate(flops=30_000_000_000, bytes_accessed=3_000_000, transcendentals=0),
        name="factor",
    )(block, *orders, panel, mask)


def panel_tile(hi, lo, pieces):
    columns = jnp.concatenate([piece[...] for piece in pieces], axis=0)
    return (fast(hi[...], columns) + fast(lo[...], columns)).astype(jnp.bfloat16)


def send_kernel(place, hi, lo, left, trailing, *rest):
    *pieces, out, right = rest

    @pl.when(pl.program_id(0) == 0)
    def _():
        right[...] = panel_tile(hi, lo, pieces)

    out[...] = (trailing[...].astype(jnp.float32) - fast(left[...], right[...])).astype(jnp.bfloat16)


def merge_kernel(place, hi, lo, left, trailing, chosen, received, *rest):
    *pieces, out, right = rest

    @pl.when(pl.program_id(0) == 0)
    def _():
        right[...] = panel_tile(hi, lo, pieces)

    own = (trailing[...].astype(jnp.float32) - fast(left[...], right[...])).astype(jnp.bfloat16)
    out[...] = (own.astype(jnp.float32) + fast(chosen[...], received[...])).astype(jnp.bfloat16)


def merge_kernel_into(place, hi, lo, left, trailing, chosen, received, *rest):
    *pieces, _, out, right = rest
    merge_kernel(place, hi, lo, left, trailing, chosen, received, *pieces, out, right)


def merge_raw_kernel(place, hi, lo, left, trailing, chosen, received, other_left, other_right, *rest):
    *pieces, out, right, updated = rest

    @pl.when(pl.program_id(0) == 0)
    def _():
        size = out.shape[0]
        for first in range(0, received.shape[0], size):
            rows = slice(first, first + size)
            update = fast(other_left[rows, :], other_right[...])
            updated[rows, :] = (received[rows, :].astype(jnp.float32) - update).astype(jnp.bfloat16)

    merge_kernel(place, hi, lo, left, trailing, chosen, updated, *pieces, out, right)


def merge_raw_kernel_into(*refs):
    merge_raw_kernel(*refs[:-4], *refs[-3:])


def specs_for(hi, left, columns, width, start, pieces, starts):
    size = hi.shape[0]
    rows = left.shape[0] // ROW_STEPS
    half_blocks, chunk = columns // 2 // width, start // width
    whole = pl.BlockSpec((size, size), lambda i, place: (0, 0))
    specs = [
        whole,
        whole,
        pl.BlockSpec((rows, size), lambda i, place: (i, 0)),
        pl.BlockSpec((rows, width), lambda i, place: (i, place[0] * half_blocks + chunk)),
    ]
    piece_specs = []
    for piece, first in zip(pieces, starts):
        block = (piece.shape[0], width)
        if first is None:
            piece_specs.append(pl.BlockSpec(block, lambda i, place: (0, place[0] * half_blocks + chunk)))
        else:
            piece_specs.append(pl.BlockSpec(block, lambda i, place, at=(start - first) // width: (0, at)))
    return specs, piece_specs


def send_chunk(place, hi, lo, left, trailing, pieces, starts, start, width):
    rows, columns = trailing.shape
    specs, piece_specs = specs_for(hi, left, columns, width, start, pieces, starts)
    return pl.pallas_call(
        send_kernel,
        grid_spec=pltpu.PrefetchScalarGridSpec(
            num_scalar_prefetch=1,
            grid=(ROW_STEPS,),
            in_specs=specs + piece_specs,
            out_specs=pl.BlockSpec((rows // ROW_STEPS, width), lambda i, place: (i, 0)),
            scratch_shapes=[pltpu.VMEM((hi.shape[0], width), jnp.bfloat16)],
        ),
        out_shape=jax.ShapeDtypeStruct((rows, width), jnp.bfloat16),
        compiler_params=pltpu.CompilerParams(vmem_limit_bytes=VMEM_LIMIT),
        cost_estimate=pl.CostEstimate(flops=2 * rows * 256 * width, bytes_accessed=5 * rows * width, transcendentals=0),
        name="send_part",
    )(place, hi, lo, left, trailing, *pieces)


def merge_chunk(place, hi, lo, left, trailing, chosen, received, pieces, starts, start, width, merged, raw=None):
    rows, columns = trailing.shape
    step_rows = rows // ROW_STEPS
    specs, piece_specs = specs_for(hi, left, columns, width, start, pieces, starts)
    specs.append(pl.BlockSpec((step_rows, rows), lambda i, place: (i, 0)))
    operands = [place, hi, lo, left, trailing, chosen, received]
    scratch = [pltpu.VMEM((hi.shape[0], width), jnp.bfloat16)]
    body, body_into = merge_kernel, merge_kernel_into
    if raw is None:
        specs.append(pl.BlockSpec((rows, width), lambda i, place: (0, 0)))
    else:
        first, other_left, other_right = raw
        at = (start - first) // width
        specs.append(pl.BlockSpec((rows, width), lambda i, place: (0, at)))
        specs.append(pl.BlockSpec(other_left.shape, lambda i, place: (0, 0)))
        specs.append(pl.BlockSpec((other_right.shape[0], width), lambda i, place: (0, at)))
        operands += [other_left, other_right]
        scratch.append(pltpu.VMEM((rows, width), jnp.bfloat16))
        body, body_into = merge_raw_kernel, merge_raw_kernel_into
    specs += piece_specs
    operands += pieces
    aliases = {}
    if merged is not None:
        aliases = {len(operands): 0}
        operands.append(merged)
        specs.append(pl.BlockSpec(memory_space=pl.ANY))
        body = body_into
    chunk = start // width
    return pl.pallas_call(
        body,
        grid_spec=pltpu.PrefetchScalarGridSpec(
            num_scalar_prefetch=1,
            grid=(ROW_STEPS,),
            in_specs=specs,
            out_specs=pl.BlockSpec((step_rows, width), lambda i, place: (i, chunk)),
            scratch_shapes=scratch,
        ),
        out_shape=jax.ShapeDtypeStruct((rows, columns // 2), jnp.bfloat16),
        input_output_aliases=aliases,
        compiler_params=pltpu.CompilerParams(vmem_limit_bytes=VMEM_LIMIT),
        cost_estimate=pl.CostEstimate(flops=2 * rows * (rows + 256) * width, bytes_accessed=8 * rows * width, transcendentals=0),
        name="merge_part",
    )(*operands)


def bits_of(axis):
    return [1 << bit for bit in reversed(range((lax.axis_size(axis) - 1).bit_length()))]


def doubled(block, axis, dimension):
    for step in range(len(bits_of(axis))):
        block = next_doubled(block, axis, dimension, step)
    return block


def next_doubled(block, axis, dimension, step):
    return jnp.concatenate([block, partner(block, axis, bits_of(axis)[step])], axis=dimension)


def place_of(index, part, axis):
    apart = (index // part) ^ lax.axis_index(axis)
    place = jnp.zeros_like(index)
    for number, bits in enumerate(bits_of(axis)):
        place = place + jnp.where(apart & bits != 0, 1 << number, 0)
    return place * part + index % part


def after(value, *others):
    return lax.optimization_barrier((value, *others))[0]


def local(diag_block, pivot_order, lower_in, upper_in, trailing, block_mask, row_map):
    diag_block, lower_in, upper_in, trailing = diag_block[0], lower_in[0], upper_in[0], trailing[0]
    size = diag_block.shape[1]
    rows, columns = trailing.shape
    half = columns // 2
    width = half // CHUNKS
    row, col = lax.axis_index("row"), lax.axis_index("col")
    parity = lax.axis_index("cube") % 2
    sent_place = (1 - parity).astype(jnp.int32).reshape(1)
    kept_place = parity.astype(jnp.int32).reshape(1)
    raw_end = RAW * width

    raw = lax.dynamic_slice_in_dim(trailing, (1 - parity) * half, raw_end, 1)
    raw_received = partner(raw, "cube", 1)

    whole_block = doubled(after(diag_block, raw), ("row", "col"), 0)
    panel = doubled(lower_in, "col", 1)
    order = pivot_order[0][:, None]
    every = jnp.arange(size, dtype=jnp.int32)
    in_row_order = place_of(every, upper_in.shape[0], "row")
    in_col_order = place_of(every, lower_in.shape[1], "col")
    orders = (
        place_of(order, diag_block.shape[0], ("row", "col")),
        place_of(order, upper_in.shape[0], "row"),
        in_col_order[None, :],
    )
    block_rows = rows // block_mask.shape[1]
    flags = block_mask[0].astype(jnp.float32)
    other_flags = partner(flags, "cube", 1)
    other_flags = jnp.where(parity == 0, other_flags[:, :1], other_flags[:, 1:])
    other_flags = jnp.repeat(other_flags, block_rows, axis=0)
    flags = jnp.repeat(flags, block_rows, axis=0)
    flags = jnp.where(parity == 0, flags[:, ::-1], flags)
    chosen = (row_map[0][:, None] == jnp.arange(rows, dtype=jnp.int32)[None, :]).astype(jnp.bfloat16)

    def columns_of(place, first, last):
        return lax.dynamic_slice_in_dim(upper_in, place * half + first, last - first, 1)

    cut = raw_end + EARLY * width
    early = doubled(columns_of(1 - parity, 0, cut), "row", 0)
    late = columns_of(1 - parity, cut, half)
    late = next_doubled(late, "row", 0, 0)

    hi, lo, plain_left, sent_left, kept_left = factor(whole_block, orders, panel, flags)

    left_share = lax.dynamic_slice_in_dim(plain_left, col * lower_in.shape[1], lower_in.shape[1], 1)
    left_received = partner(left_share, "cube", 1)
    share = upper_in.shape[0]
    share_hi = lax.dynamic_slice_in_dim(hi, row * share, share, 0)
    share_lo = lax.dynamic_slice_in_dim(lo, row * share, share, 0)
    same = (in_col_order[:, None, None] == jnp.arange(size)[None, :, None]) & (
        in_row_order[:, None, None] == jnp.arange(size)[None, None, :]
    )
    same = jnp.any(same, axis=0).astype(jnp.bfloat16)

    bounds = [width * chunk for chunk in range(RAW, CHUNKS + 1)]
    if width % 256 == 0:
        bounds.insert(-1, half - width // 2)
    spans = list(zip(bounds, bounds[1:]))
    sent, received, merged_after = [], [], []
    merged = None

    def merge(number):
        start, end = spans[number]
        return merge_chunk(
            kept_place, hi, lo, kept_left, trailing, chosen, received[number], [kept_upper], [0], start, end - start,
            merged,
        )

    for number, (start, end) in enumerate(spans):
        before = []
        if number >= AHEAD - 1:
            before += [([raw_received] + received)[number - AHEAD + 1], sent[-1]]
        if number == 1:
            for step in range(1, len(bits_of("row"))):
                late = next_doubled(after(late, sent[0]), "row", 0, step)
        if number == 2:
            kept_upper = next_doubled(after(columns_of(parity, 0, half), raw_received), "row", 0, 0)
        if number == 3:
            before += [left_received]
            raw_upper = after(early[:, :raw_end], received[0])
            right_share = (fast(share_hi, raw_upper) + fast(share_lo, raw_upper)).astype(jnp.bfloat16)
            right_received = partner(right_share, "cube", 1)
        if number == 4:
            before += [kept_upper]
            for step in range(1, len(bits_of("row"))):
                kept_upper = next_doubled(after(kept_upper, received[1]), "row", 0, step)
        if number == 5:
            before += [right_received]
            other_left = doubled(after(left_received, received[2]), "col", 1)
            other_left = (fast(other_left, same) * other_flags).astype(jnp.bfloat16)
        if number == 6:
            before += [kept_upper]
            other_right = doubled(after(right_received, received[3]), "row", 0)
        if number == 7:
            before += [other_left, other_right]
        if number >= BEHIND:
            merged = merge(number - BEHIND)
            before += [merged]
        place = after(sent_place, *before) if before else sent_place
        piece, first = (early, 0) if end <= cut else (late, cut)
        sent.append(send_chunk(place, hi, lo, sent_left, trailing, [piece], [first], start, end - start))
        received.append(partner(sent[-1], "cube", 1))

    for start in range(0, raw_end, width):
        merged = merge_chunk(
            kept_place, hi, lo, kept_left, trailing, chosen, raw_received, [kept_upper], [0], start, width, merged,
            (0, other_left, other_right),
        )
    for number in range(len(spans) - BEHIND, len(spans)):
        merged = merge(number)
    return merged[None]


def solution(mesh):
    return jax.shard_map(
        local,
        mesh=mesh,
        in_specs=(
            P("cube", ("row", "col"), None),
            P("cube", None),
            P("cube", "row", "col"),
            P("cube", "row", "col"),
            P("cube", "row", "col"),
            P("cube", "row", "col"),
            P("cube", "row"),
        ),
        out_specs=P("cube", "row", "col"),
        check_vma=False,
    )
```

```python
import functools

import jax
import jax.numpy as jnp
from jax import lax
from jax.experimental import pallas as pl
from jax.experimental.pallas import tpu as pltpu
from jax.sharding import PartitionSpec as P

CHUNKS = 15
RAW = 2
EARLY = 2
AHEAD = 3
BEHIND = 6
ROW_STEPS = 4
HIGH = lax.Precision.HIGHEST
VMEM_LIMIT = 48 * 1024 * 1024


def partner(block, axis, bits):
    count = lax.axis_size(axis)
    return lax.ppermute(block, axis, [(i, i ^ bits) for i in range(count)])


def exact(left, right):
    return jnp.dot(left, right, precision=HIGH, preferred_element_type=jnp.float32)


def fast(left, right):
    return jnp.dot(left, right, preferred_element_type=jnp.float32)


def split(value):
    high = value.astype(jnp.bfloat16)
    return high, (value - high.astype(jnp.float32)).astype(jnp.bfloat16)


def eliminate(block):
    size = block.shape[0]
    row = lax.broadcasted_iota(jnp.int32, (size, size), 0)
    lane = lax.broadcasted_iota(jnp.int32, (size, size), 1)

    def eight(turn, work):
        left = size - 8 * turn
        for step in range(8):
            column = work[:, step : step + 1]
            pivot_row = work[step : step + 1, :]
            inverse = 1.0 / work[step : step + 1, step : step + 1]
            scaled = pivot_row * inverse
            lane_one = lane[:1]
            at = lane_one == step
            passed = (lane_one < step) | (lane_one >= left)
            for_later = jnp.where(at, inverse, scaled)
            for_passed = jnp.where(passed | at, 0.0, scaled)
            row_passed = (row < step) | (row >= left)
            base = jnp.where((lane == step) & jnp.logical_not(row_passed), 0.0, work)
            fresh = base - column * jnp.where(row_passed, for_passed, for_later)
            own = jnp.where(at, inverse, jnp.where(passed, pivot_row, -scaled))
            work = jnp.where(row == step, own, fresh)
        work = jnp.concatenate([work[8:], work[:8]], axis=0)
        return pltpu.roll(work, size - 8, 1)

    return lax.fori_loop(0, size // 8, eight, block)


def inverses(block):
    size = block.shape[0]
    work = eliminate(block)
    row = lax.broadcasted_iota(jnp.int32, (size, size), 0)
    lane = lax.broadcasted_iota(jnp.int32, (size, size), 1)
    diagonal = jnp.sum(jnp.where(row == lane, work, 0.0), axis=0, keepdims=True)
    lower = jnp.where(row > lane, work, jnp.where(row == lane, 1.0, 0.0))
    upper = jnp.where(row < lane, work * diagonal, jnp.where(row == lane, work, 0.0))
    return lower, upper


def factor_kernel(block, order_of_diag, order_of_upper, order_of_lower, panel, mask, hi, lo, plain, sent, kept):
    size = block.shape[0]
    half = size // 2
    lane = lax.broadcasted_iota(jnp.int32, (size, size), 1)

    def chosen(order):
        return jnp.where(order[...] == lane, 1.0, 0.0)

    pivoted = exact(chosen(order_of_diag), block[...])
    lower_one, upper_one = inverses(pivoted[:half, :half])
    lower_side = exact(pivoted[half:, :half], upper_one)
    upper_side = exact(lower_one, pivoted[:half, half:])
    schur = pivoted[half:, half:] - exact(lower_side, upper_side)
    lower_two, upper_two = inverses(schur)
    zero = jnp.zeros((half, half), jnp.float32)
    corner_lower = -exact(lower_two, exact(lower_side, lower_one))
    corner_upper = -exact(upper_one, exact(upper_side, upper_two))
    lower_inv = jnp.concatenate(
        [jnp.concatenate([lower_one, zero], 1), jnp.concatenate([corner_lower, lower_two], 1)], 0
    )
    upper_inv = jnp.concatenate(
        [jnp.concatenate([upper_one, corner_upper], 1), jnp.concatenate([zero, upper_two], 1)], 0
    )
    hi[...], lo[...] = split(exact(lower_inv, chosen(order_of_upper)))
    row = lax.broadcasted_iota(jnp.int32, (size, size), 0)
    in_order = jnp.where(order_of_lower[...] == row, 1.0, 0.0)
    upper_hi, upper_lo = split(exact(in_order, upper_inv))
    for start in range(0, panel.shape[0], size):
        rows = slice(start, start + size)
        part = panel[rows, :]
        result = fast(part, upper_hi) + fast(part, upper_lo)
        plain[rows, :] = result.astype(jnp.bfloat16)
        result = result.astype(jnp.bfloat16).astype(jnp.float32)
        sent[rows, :] = (result * mask[rows, 0:1]).astype(jnp.bfloat16)
        kept[rows, :] = (result * mask[rows, 1:2]).astype(jnp.bfloat16)


def factor(block, orders, panel, mask):
    size = block.shape[0]
    rows = panel.shape[0]
    half_type = jnp.bfloat16
    return pl.pallas_call(
        factor_kernel,
        out_shape=(
            jax.ShapeDtypeStruct((size, size), half_type),
            jax.ShapeDtypeStruct((size, size), half_type),
            jax.ShapeDtypeStruct((rows, size), half_type),
            jax.ShapeDtypeStruct((rows, size), half_type),
            jax.ShapeDtypeStruct((rows, size), half_type),
        ),
        compiler_params=pltpu.CompilerParams(vmem_limit_bytes=VMEM_LIMIT),
        cost_estimate=pl.CostEstimate(flops=30_000_000_000, bytes_accessed=3_000_000, transcendentals=0),
        name="factor",
    )(block, *orders, panel, mask)


def panel_tile(hi, lo, pieces):
    columns = jnp.concatenate([piece[...] for piece in pieces], axis=0)
    return (fast(hi[...], columns) + fast(lo[...], columns)).astype(jnp.bfloat16)


def send_kernel(place, hi, lo, left, trailing, *rest):
    *pieces, out, right = rest

    @pl.when(pl.program_id(0) == 0)
    def _():
        right[...] = panel_tile(hi, lo, pieces)

    out[...] = (trailing[...].astype(jnp.float32) - fast(left[...], right[...])).astype(jnp.bfloat16)


def merge_kernel(place, hi, lo, left, trailing, chosen, received, *rest):
    *pieces, out, right = rest

    @pl.when(pl.program_id(0) == 0)
    def _():
        right[...] = panel_tile(hi, lo, pieces)

    own = (trailing[...].astype(jnp.float32) - fast(left[...], right[...])).astype(jnp.bfloat16)
    out[...] = (own.astype(jnp.float32) + fast(chosen[...], received[...])).astype(jnp.bfloat16)


def merge_kernel_into(place, hi, lo, left, trailing, chosen, received, *rest):
    *pieces, _, out, right = rest
    merge_kernel(place, hi, lo, left, trailing, chosen, received, *pieces, out, right)


def merge_raw_kernel(place, hi, lo, left, trailing, chosen, received, other_left, other_right, *rest):
    *pieces, out, right, updated = rest

    @pl.when(pl.program_id(0) == 0)
    def _():
        size = out.shape[0]
        for first in range(0, received.shape[0], size):
            rows = slice(first, first + size)
            update = fast(other_left[rows, :], other_right[...])
            updated[rows, :] = (received[rows, :].astype(jnp.float32) - update).astype(jnp.bfloat16)

    merge_kernel(place, hi, lo, left, trailing, chosen, updated, *pieces, out, right)


def merge_raw_kernel_into(*refs):
    merge_raw_kernel(*refs[:-4], *refs[-3:])


def specs_for(hi, left, columns, width, start, pieces, starts):
    size = hi.shape[0]
    rows = left.shape[0] // ROW_STEPS
    half_blocks, chunk = columns // 2 // width, start // width
    whole = pl.BlockSpec((size, size), lambda i, place: (0, 0))
    specs = [
        whole,
        whole,
        pl.BlockSpec((rows, size), lambda i, place: (i, 0)),
        pl.BlockSpec((rows, width), lambda i, place: (i, place[0] * half_blocks + chunk)),
    ]
    piece_specs = []
    for piece, first in zip(pieces, starts):
        block = (piece.shape[0], width)
        if first is None:
            piece_specs.append(pl.BlockSpec(block, lambda i, place: (0, place[0] * half_blocks + chunk)))
        else:
            piece_specs.append(pl.BlockSpec(block, lambda i, place, at=(start - first) // width: (0, at)))
    return specs, piece_specs


def send_chunk(place, hi, lo, left, trailing, pieces, starts, start, width):
    rows, columns = trailing.shape
    specs, piece_specs = specs_for(hi, left, columns, width, start, pieces, starts)
    return pl.pallas_call(
        send_kernel,
        grid_spec=pltpu.PrefetchScalarGridSpec(
            num_scalar_prefetch=1,
            grid=(ROW_STEPS,),
            in_specs=specs + piece_specs,
            out_specs=pl.BlockSpec((rows // ROW_STEPS, width), lambda i, place: (i, 0)),
            scratch_shapes=[pltpu.VMEM((hi.shape[0], width), jnp.bfloat16)],
        ),
        out_shape=jax.ShapeDtypeStruct((rows, width), jnp.bfloat16),
        compiler_params=pltpu.CompilerParams(vmem_limit_bytes=VMEM_LIMIT),
        cost_estimate=pl.CostEstimate(flops=2 * rows * 256 * width, bytes_accessed=5 * rows * width, transcendentals=0),
        name="send_part",
    )(place, hi, lo, left, trailing, *pieces)


def merge_chunk(place, hi, lo, left, trailing, chosen, received, pieces, starts, start, width, merged, raw=None):
    rows, columns = trailing.shape
    step_rows = rows // ROW_STEPS
    specs, piece_specs = specs_for(hi, left, columns, width, start, pieces, starts)
    specs.append(pl.BlockSpec((step_rows, rows), lambda i, place: (i, 0)))
    operands = [place, hi, lo, left, trailing, chosen, received]
    scratch = [pltpu.VMEM((hi.shape[0], width), jnp.bfloat16)]
    body, body_into = merge_kernel, merge_kernel_into
    if raw is None:
        specs.append(pl.BlockSpec((rows, width), lambda i, place: (0, 0)))
    else:
        first, other_left, other_right = raw
        at = (start - first) // width
        specs.append(pl.BlockSpec((rows, width), lambda i, place: (0, at)))
        specs.append(pl.BlockSpec(other_left.shape, lambda i, place: (0, 0)))
        specs.append(pl.BlockSpec((other_right.shape[0], width), lambda i, place: (0, at)))
        operands += [other_left, other_right]
        scratch.append(pltpu.VMEM((rows, width), jnp.bfloat16))
        body, body_into = merge_raw_kernel, merge_raw_kernel_into
    specs += piece_specs
    operands += pieces
    aliases = {}
    if merged is not None:
        aliases = {len(operands): 0}
        operands.append(merged)
        specs.append(pl.BlockSpec(memory_space=pl.ANY))
        body = body_into
    chunk = start // width
    return pl.pallas_call(
        body,
        grid_spec=pltpu.PrefetchScalarGridSpec(
            num_scalar_prefetch=1,
            grid=(ROW_STEPS,),
            in_specs=specs,
            out_specs=pl.BlockSpec((step_rows, width), lambda i, place: (i, chunk)),
            scratch_shapes=scratch,
        ),
        out_shape=jax.ShapeDtypeStruct((rows, columns // 2), jnp.bfloat16),
        input_output_aliases=aliases,
        compiler_params=pltpu.CompilerParams(vmem_limit_bytes=VMEM_LIMIT),
        cost_estimate=pl.CostEstimate(flops=2 * rows * (rows + 256) * width, bytes_accessed=8 * rows * width, transcendentals=0),
        name="merge_part",
    )(*operands)


def join_kernel(own, received, _, out):
    out[...] = (own[...].astype(jnp.float32) + received[...].astype(jnp.float32)).astype(jnp.bfloat16)


def join_chunk(own, received, start, merged):
    rows, width = own.shape
    step_rows = rows // 2
    part = pl.BlockSpec((step_rows, width), lambda i: (i, 0))
    return pl.pallas_call(
        join_kernel,
        grid=(2,),
        in_specs=[part, part, pl.BlockSpec(memory_space=pl.ANY)],
        out_specs=pl.BlockSpec((step_rows, width), lambda i: (i, start // width)),
        out_shape=jax.ShapeDtypeStruct(merged.shape, merged.dtype),
        input_output_aliases={2: 0},
        compiler_params=pltpu.CompilerParams(vmem_limit_bytes=VMEM_LIMIT),
        cost_estimate=pl.CostEstimate(flops=rows * width, bytes_accessed=6 * rows * width, transcendentals=0),
        name="join_part",
    )(own, received, merged)


def bits_of(axis):
    return [1 << bit for bit in reversed(range((lax.axis_size(axis) - 1).bit_length()))]


def doubled(block, axis, dimension):
    for step in range(len(bits_of(axis))):
        block = next_doubled(block, axis, dimension, step)
    return block


def next_doubled(block, axis, dimension, step):
    return jnp.concatenate([block, partner(block, axis, bits_of(axis)[step])], axis=dimension)


def place_of(index, part, axis):
    apart = (index // part) ^ lax.axis_index(axis)
    place = jnp.zeros_like(index)
    for number, bits in enumerate(bits_of(axis)):
        place = place + jnp.where(apart & bits != 0, 1 << number, 0)
    return place * part + index % part


def index_at(place, part, axis):
    number = place // part
    apart = jnp.zeros_like(place)
    for bit, bits in enumerate(bits_of(axis)):
        apart = apart + jnp.where(number & (1 << bit) != 0, bits, 0)
    return (apart ^ lax.axis_index(axis)) * part + place % part


def after(value, *others):
    return lax.optimization_barrier((value, *others))[0]


def local(diag_block, pivot_order, lower_in, upper_in, trailing, block_mask, row_map):
    diag_block, lower_in, upper_in, trailing = diag_block[0], lower_in[0], upper_in[0], trailing[0]
    size = diag_block.shape[1]
    rows, columns = trailing.shape
    half = columns // 2
    width = half // CHUNKS
    row, col = lax.axis_index("row"), lax.axis_index("col")
    parity = lax.axis_index("cube") % 2
    sent_place = (1 - parity).astype(jnp.int32).reshape(1)
    kept_place = parity.astype(jnp.int32).reshape(1)
    raw_end = RAW * width

    raw = lax.dynamic_slice_in_dim(trailing, (1 - parity) * half, raw_end, 1)
    raw_received = partner(raw, "cube", 1)

    whole_block = doubled(after(diag_block, raw), ("row", "col"), 0)
    panel = doubled(lower_in, "col", 1)
    order = pivot_order[0][:, None]
    every = jnp.arange(size, dtype=jnp.int32)
    in_col_order = place_of(every, lower_in.shape[1], "col")
    orders = (
        place_of(order, diag_block.shape[0], ("row", "col")),
        place_of(order, upper_in.shape[0], "row"),
        in_col_order[None, :],
    )
    block_rows = rows // block_mask.shape[1]
    flags = block_mask[0].astype(jnp.float32)
    own_flags = flags
    flags = jnp.repeat(flags, block_rows, axis=0)
    flags = jnp.where(parity == 0, flags[:, ::-1], flags)
    def columns_of(place, first, last):
        return lax.dynamic_slice_in_dim(upper_in, place * half + first, last - first, 1)

    cut = raw_end + EARLY * width
    early = doubled(columns_of(1 - parity, 0, cut), "row", 0)
    late = columns_of(1 - parity, cut, half)
    late = next_doubled(late, "row", 0, 0)

    hi, lo, plain_left, sent_left, kept_left = factor(whole_block, orders, panel, flags)

    left_share = lax.dynamic_slice_in_dim(plain_left, col * lower_in.shape[1], lower_in.shape[1], 1)
    left_received = partner(left_share, "cube", 1)
    share = upper_in.shape[0]
    share_hi = lax.dynamic_slice_in_dim(hi, row * share, share, 0)
    share_lo = lax.dynamic_slice_in_dim(lo, row * share, share, 0)
    col_order = index_at(every, lower_in.shape[1], "col")
    row_order = index_at(every, upper_in.shape[0], "row")
    same = (after(col_order, hi)[:, None] == row_order[None, :]).astype(jnp.bfloat16)

    def choice(order):
        return (order[:, None] == jnp.arange(rows, dtype=jnp.int32)[None, :]).astype(jnp.bfloat16)

    chosen = choice(after(row_map[0], hi))

    bounds = [width * chunk for chunk in range(RAW, CHUNKS + 1)]
    if width % 256 == 0:
        bounds.insert(-1, half - width // 2)
    spans = list(zip(bounds, bounds[1:]))
    sent, received, merged_after = [], [], []
    merged = None

    def merge(number):
        start, end = spans[number]
        return merge_chunk(
            kept_place, hi, lo, kept_left, trailing, chosen, received[number], [kept_upper], [0], start, end - start,
            merged,
        )

    for number, (start, end) in enumerate(spans):
        before = []
        if number >= AHEAD - 1:
            before += [([raw_received] + received)[number - AHEAD + 1], sent[-1]]
        if number == 1:
            for step in range(1, len(bits_of("row"))):
                late = next_doubled(after(late, sent[0]), "row", 0, step)
        if number == 2:
            kept_upper = next_doubled(after(columns_of(parity, 0, half), raw_received, sent[1]), "row", 0, 0)
        if number == 3:
            before += [left_received]
            raw_upper = after(early[:, :raw_end], received[0], sent[2])
            right_share = (fast(share_hi, raw_upper) + fast(share_lo, raw_upper)).astype(jnp.bfloat16)
            right_received = partner(right_share, "cube", 1)
        if number == 4:
            before += [kept_upper]
            for step in range(1, len(bits_of("row"))):
                kept_upper = next_doubled(after(kept_upper, received[1], sent[3]), "row", 0, step)
        if number == 5:
            before += [right_received]
            other_left = doubled(after(left_received, received[2], sent[4]), "col", 1)
        if number == 6:
            before += [kept_upper]
            other_right = doubled(after(right_received, received[3], sent[5]), "row", 0)
        if number == 7:
            before += [other_left, other_right]
        if number == 9:
            other_flags = jnp.where(parity == 0, other_flags[:, :1], other_flags[:, 1:])
            other_left = fast(other_left, same) * jnp.repeat(other_flags, block_rows, axis=0)
            other_left = other_left.astype(jnp.bfloat16)
        if number == 10:
            before += [other_chosen, other_left]
        if number == 8:
            other_flags = partner(after(own_flags, received[5], sent[7]), "cube", 1)
            other_chosen = choice(partner(after(row_map[0], received[5], sent[7]), "cube", 1))
        if number >= BEHIND:
            merged = merge(number - BEHIND)
            before += [merged]
        place = after(sent_place, *before) if before else sent_place
        piece, first = (early, 0) if end <= cut else (late, cut)
        sent.append(send_chunk(place, hi, lo, sent_left, trailing, [piece], [first], start, end - start))
        outgoing = sent[-1]
        if number == len(spans) - 1:
            outgoing = fast(other_chosen, outgoing).astype(jnp.bfloat16)
        received.append(partner(outgoing, "cube", 1))

    for start in range(0, raw_end, width):
        merged = merge_chunk(
            kept_place, hi, lo, kept_left, trailing, chosen, raw_received, [kept_upper], [0], start, width, merged,
            (0, other_left, other_right),
        )
    for number in range(len(spans) - BEHIND, len(spans) - 1):
        merged = merge(number)
    start, end = spans[-1]
    own = send_chunk(
        after(kept_place, merged), hi, lo, kept_left, trailing, [kept_upper], [0], start, end - start
    )
    merged = join_chunk(own, received[-1], start, merged)
    return merged[None]


def solution(mesh):
    return jax.shard_map(
        local,
        mesh=mesh,
        in_specs=(
            P("cube", ("row", "col"), None),
            P("cube", None),
            P("cube", "row", "col"),
            P("cube", "row", "col"),
            P("cube", "row", "col"),
            P("cube", "row", "col"),
            P("cube", "row"),
        ),
        out_specs=P("cube", "row", "col"),
        check_vma=False,
    )
```

```python
import functools

import jax
import jax.numpy as jnp
from jax import lax
from jax.experimental import pallas as pl
from jax.experimental.pallas import tpu as pltpu
from jax.sharding import PartitionSpec as P

CHUNKS = 15
RAW = 2
EARLY = 3
PARTS = (2, 3, 5, 7, 9, 11, 13, 14, 15)
EVEN_PARTS = (2, 3, 5, 7, 9, 11, 12, 13, 14, 15)
AHEAD = 3
MERGES = {6: (0,), 7: (1, 2), 8: (3, 4)}
ROW_STEPS = 4
HIGH = lax.Precision.HIGHEST
VMEM_LIMIT = 48 * 1024 * 1024


def partner(block, axis, bits):
    count = lax.axis_size(axis)
    return lax.ppermute(block, axis, [(i, i ^ bits) for i in range(count)])


def exact(left, right):
    return jnp.dot(left, right, precision=HIGH, preferred_element_type=jnp.float32)


def fast(left, right):
    return jnp.dot(left, right, preferred_element_type=jnp.float32)


def split(value):
    high = value.astype(jnp.bfloat16)
    return high, (value - high.astype(jnp.float32)).astype(jnp.bfloat16)


def eliminate(block):
    size = block.shape[0]
    row = lax.broadcasted_iota(jnp.int32, (size, size), 0)
    lane = lax.broadcasted_iota(jnp.int32, (size, size), 1)

    def eight(turn, work):
        left = size - 8 * turn
        for step in range(8):
            column = work[:, step : step + 1]
            pivot_row = work[step : step + 1, :]
            inverse = 1.0 / work[step : step + 1, step : step + 1]
            scaled = pivot_row * inverse
            lane_one = lane[:1]
            at = lane_one == step
            passed = (lane_one < step) | (lane_one >= left)
            for_later = jnp.where(at, inverse, scaled)
            for_passed = jnp.where(passed | at, 0.0, scaled)
            row_passed = (row < step) | (row >= left)
            base = jnp.where((lane == step) & jnp.logical_not(row_passed), 0.0, work)
            fresh = base - column * jnp.where(row_passed, for_passed, for_later)
            own = jnp.where(at, inverse, jnp.where(passed, pivot_row, -scaled))
            work = jnp.where(row == step, own, fresh)
        work = jnp.concatenate([work[8:], work[:8]], axis=0)
        return pltpu.roll(work, size - 8, 1)

    return lax.fori_loop(0, size // 8, eight, block)


def inverses(block):
    size = block.shape[0]
    work = eliminate(block)
    row = lax.broadcasted_iota(jnp.int32, (size, size), 0)
    lane = lax.broadcasted_iota(jnp.int32, (size, size), 1)
    diagonal = jnp.sum(jnp.where(row == lane, work, 0.0), axis=0, keepdims=True)
    lower = jnp.where(row > lane, work, jnp.where(row == lane, 1.0, 0.0))
    upper = jnp.where(row < lane, work * diagonal, jnp.where(row == lane, work, 0.0))
    return lower, upper


def factor_kernel(block, order_of_diag, order_of_upper, order_of_lower, panel, mask, hi, lo, plain, sent, kept):
    size = block.shape[0]
    half = size // 2
    lane = lax.broadcasted_iota(jnp.int32, (size, size), 1)

    def chosen(order):
        return jnp.where(order[...] == lane, 1.0, 0.0)

    pivoted = exact(chosen(order_of_diag), block[...])
    lower_one, upper_one = inverses(pivoted[:half, :half])
    lower_side = exact(pivoted[half:, :half], upper_one)
    upper_side = exact(lower_one, pivoted[:half, half:])
    schur = pivoted[half:, half:] - exact(lower_side, upper_side)
    lower_two, upper_two = inverses(schur)
    zero = jnp.zeros((half, half), jnp.float32)
    corner_lower = -exact(lower_two, exact(lower_side, lower_one))
    corner_upper = -exact(upper_one, exact(upper_side, upper_two))
    lower_inv = jnp.concatenate(
        [jnp.concatenate([lower_one, zero], 1), jnp.concatenate([corner_lower, lower_two], 1)], 0
    )
    upper_inv = jnp.concatenate(
        [jnp.concatenate([upper_one, corner_upper], 1), jnp.concatenate([zero, upper_two], 1)], 0
    )
    hi[...], lo[...] = split(exact(lower_inv, chosen(order_of_upper)))
    row = lax.broadcasted_iota(jnp.int32, (size, size), 0)
    in_order = jnp.where(order_of_lower[...] == row, 1.0, 0.0)
    upper_hi, upper_lo = split(exact(in_order, upper_inv))
    for start in range(0, panel.shape[0], size):
        rows = slice(start, start + size)
        part = panel[rows, :]
        result = fast(part, upper_hi) + fast(part, upper_lo)
        plain[rows, :] = result.astype(jnp.bfloat16)
        result = result.astype(jnp.bfloat16).astype(jnp.float32)
        sent[rows, :] = (result * mask[rows, 0:1]).astype(jnp.bfloat16)
        kept[rows, :] = (result * mask[rows, 1:2]).astype(jnp.bfloat16)


def factor(block, orders, panel, mask):
    size = block.shape[0]
    rows = panel.shape[0]
    half_type = jnp.bfloat16
    return pl.pallas_call(
        factor_kernel,
        out_shape=(
            jax.ShapeDtypeStruct((size, size), half_type),
            jax.ShapeDtypeStruct((size, size), half_type),
            jax.ShapeDtypeStruct((rows, size), half_type),
            jax.ShapeDtypeStruct((rows, size), half_type),
            jax.ShapeDtypeStruct((rows, size), half_type),
        ),
        compiler_params=pltpu.CompilerParams(vmem_limit_bytes=VMEM_LIMIT),
        cost_estimate=pl.CostEstimate(flops=30_000_000_000, bytes_accessed=3_000_000, transcendentals=0),
        name="factor",
    )(block, *orders, panel, mask)


def panel_tile(hi, lo, pieces):
    columns = jnp.concatenate([piece[...] for piece in pieces], axis=0)
    return (fast(hi[...], columns) + fast(lo[...], columns)).astype(jnp.bfloat16)


def send_kernel(place, hi, lo, left, trailing, *rest):
    *pieces, out, right = rest

    @pl.when(pl.program_id(1) == 0)
    def _():
        right[...] = panel_tile(hi, lo, pieces)

    out[...] = (trailing[...].astype(jnp.float32) - fast(left[...], right[...])).astype(jnp.bfloat16)


def merge_kernel(place, hi, lo, left, trailing, chosen, received, *rest):
    *pieces, out, right = rest

    @pl.when(pl.program_id(1) == 0)
    def _():
        right[...] = panel_tile(hi, lo, pieces)

    own = (trailing[...].astype(jnp.float32) - fast(left[...], right[...])).astype(jnp.bfloat16)
    out[...] = (own.astype(jnp.float32) + fast(chosen[...], received[...])).astype(jnp.bfloat16)


def merge_kernel_into(place, hi, lo, left, trailing, chosen, received, *rest):
    *pieces, _, out, right = rest
    merge_kernel(place, hi, lo, left, trailing, chosen, received, *pieces, out, right)


def merge_raw_kernel(place, hi, lo, left, trailing, chosen, received, other_left, other_right, *rest):
    *pieces, out, right, updated = rest

    @pl.when(pl.program_id(1) == 0)
    def _():
        size = out.shape[0]
        for first in range(0, received.shape[0], size):
            rows = slice(first, first + size)
            update = fast(other_left[rows, :], other_right[...])
            updated[rows, :] = (received[rows, :].astype(jnp.float32) - update).astype(jnp.bfloat16)

    merge_kernel(place, hi, lo, left, trailing, chosen, updated, *pieces, out, right)


def merge_raw_kernel_into(*refs):
    merge_raw_kernel(*refs[:-4], *refs[-3:])


def specs_for(hi, left, columns, width, start, pieces, starts):
    size = hi.shape[0]
    rows = left.shape[0] // ROW_STEPS
    half_blocks, chunk = columns // 2 // width, start // width
    whole = pl.BlockSpec((size, size), lambda j, i, place: (0, 0))
    specs = [
        whole,
        whole,
        pl.BlockSpec((rows, size), lambda j, i, place: (i, 0)),
        pl.BlockSpec((rows, width), lambda j, i, place: (i, place[0] * half_blocks + chunk + j)),
    ]
    piece_specs = [
        pl.BlockSpec((piece.shape[0], width), lambda j, i, place, at=(start - first) // width: (0, at + j))
        for piece, first in zip(pieces, starts)
    ]
    return specs, piece_specs


def cost(rows, width, flops, passes):
    return pl.CostEstimate(flops=flops * rows * width, bytes_accessed=passes * rows * width, transcendentals=0)


def send_chunk(place, hi, lo, left, trailing, pieces, starts, start, end, width):
    rows, columns = trailing.shape
    specs, piece_specs = specs_for(hi, left, columns, width, start, pieces, starts)
    return pl.pallas_call(
        send_kernel,
        grid_spec=pltpu.PrefetchScalarGridSpec(
            num_scalar_prefetch=1,
            grid=((end - start) // width, ROW_STEPS),
            in_specs=specs + piece_specs,
            out_specs=pl.BlockSpec((rows // ROW_STEPS, width), lambda j, i, place: (i, j)),
            scratch_shapes=[pltpu.VMEM((hi.shape[0], width), jnp.bfloat16)],
        ),
        out_shape=jax.ShapeDtypeStruct((rows, end - start), jnp.bfloat16),
        compiler_params=pltpu.CompilerParams(vmem_limit_bytes=VMEM_LIMIT),
        cost_estimate=cost(rows, end - start, 512, 5),
        name="send_part",
    )(place, hi, lo, left, trailing, *pieces)


def merge_chunk(
    place, hi, lo, left, trailing, chosen, received, pieces, starts, start, end, width, merged, raw=None
):
    rows, columns = trailing.shape
    step_rows = rows // ROW_STEPS
    specs, piece_specs = specs_for(hi, left, columns, width, start, pieces, starts)
    specs.append(pl.BlockSpec((step_rows, rows), lambda j, i, place: (i, 0)))
    specs.append(pl.BlockSpec((rows, width), lambda j, i, place: (0, j)))
    operands = [place, hi, lo, left, trailing, chosen, received]
    scratch = [pltpu.VMEM((hi.shape[0], width), jnp.bfloat16)]
    body, body_into = merge_kernel, merge_kernel_into
    chunk = start // width
    if raw is not None:
        other_left, other_right = raw
        specs.append(pl.BlockSpec(other_left.shape, lambda j, i, place: (0, 0)))
        specs.append(pl.BlockSpec((other_right.shape[0], width), lambda j, i, place: (0, chunk + j)))
        operands += [other_left, other_right]
        scratch.append(pltpu.VMEM((rows, width), jnp.bfloat16))
        body, body_into = merge_raw_kernel, merge_raw_kernel_into
    specs += piece_specs
    operands += pieces
    aliases = {}
    if merged is not None:
        aliases = {len(operands): 0}
        operands.append(merged)
        specs.append(pl.BlockSpec(memory_space=pl.ANY))
        body = body_into
    return pl.pallas_call(
        body,
        grid_spec=pltpu.PrefetchScalarGridSpec(
            num_scalar_prefetch=1,
            grid=((end - start) // width, ROW_STEPS),
            in_specs=specs,
            out_specs=pl.BlockSpec((step_rows, width), lambda j, i, place: (i, chunk + j)),
            scratch_shapes=scratch,
        ),
        out_shape=jax.ShapeDtypeStruct((rows, columns // 2), jnp.bfloat16),
        input_output_aliases=aliases,
        compiler_params=pltpu.CompilerParams(vmem_limit_bytes=VMEM_LIMIT),
        cost_estimate=cost(rows, end - start, 2560, 8),
        name="merge_part",
    )(*operands)


def join_kernel(own, received, _, out):
    out[...] = (own[...].astype(jnp.float32) + received[...].astype(jnp.float32)).astype(jnp.bfloat16)


def join_chunk(own, received, start, merged):
    rows, width = own.shape
    step_rows = rows // 2
    part = pl.BlockSpec((step_rows, width), lambda i: (i, 0))
    return pl.pallas_call(
        join_kernel,
        grid=(2,),
        in_specs=[part, part, pl.BlockSpec(memory_space=pl.ANY)],
        out_specs=pl.BlockSpec((step_rows, width), lambda i: (i, start // width)),
        out_shape=jax.ShapeDtypeStruct(merged.shape, merged.dtype),
        input_output_aliases={2: 0},
        compiler_params=pltpu.CompilerParams(vmem_limit_bytes=VMEM_LIMIT),
        cost_estimate=cost(rows, width, 1, 6),
        name="join_part",
    )(own, received, merged)


def bits_of(axis):
    return [1 << bit for bit in reversed(range((lax.axis_size(axis) - 1).bit_length()))]


def doubled(block, axis, dimension):
    for step in range(len(bits_of(axis))):
        block = next_doubled(block, axis, dimension, step)
    return block


def next_doubled(block, axis, dimension, step):
    return jnp.concatenate([block, partner(block, axis, bits_of(axis)[step])], axis=dimension)


def place_of(index, part, axis):
    apart = (index // part) ^ lax.axis_index(axis)
    place = jnp.zeros_like(index)
    for number, bits in enumerate(bits_of(axis)):
        place = place + jnp.where(apart & bits != 0, 1 << number, 0)
    return place * part + index % part


def index_at(place, part, axis):
    number = place // part
    apart = jnp.zeros_like(place)
    for bit, bits in enumerate(bits_of(axis)):
        apart = apart + jnp.where(number & (1 << bit) != 0, bits, 0)
    return (apart ^ lax.axis_index(axis)) * part + place % part


def after(value, *others):
    return lax.optimization_barrier((value, *others))[0]


def local(diag_block, pivot_order, lower_in, upper_in, trailing, block_mask, row_map):
    diag_block, lower_in, upper_in, trailing = diag_block[0], lower_in[0], upper_in[0], trailing[0]
    size = diag_block.shape[1]
    rows, columns = trailing.shape
    half = columns // 2
    width = half // CHUNKS
    row, col = lax.axis_index("row"), lax.axis_index("col")
    parity = lax.axis_index("cube") % 2
    sent_place = (1 - parity).astype(jnp.int32).reshape(1)
    kept_place = parity.astype(jnp.int32).reshape(1)
    raw_end = RAW * width

    raw_width = width // 2 if width % 256 == 0 else width
    raw_bounds = (0, raw_width, raw_end)
    small = jnp.concatenate([row_map[0], block_mask[0].reshape(-1)])
    other_small = partner(small, "cube", 1)
    raw = [
        lax.dynamic_slice_in_dim(
            trailing if first == 0 else after(trailing, other_small), (1 - parity) * half + first, last - first, 1
        )
        for first, last in zip(raw_bounds, raw_bounds[1:])
    ]
    raw_received = [partner(piece, "cube", 1) for piece in raw]

    whole_block = doubled(after(diag_block, raw[0]), ("row", "col"), 0)
    panel = after(doubled(lower_in, "col", 1), raw_received[0])
    order = pivot_order[0][:, None]
    every = jnp.arange(size, dtype=jnp.int32)
    in_col_order = place_of(every, lower_in.shape[1], "col")
    orders = (
        place_of(order, diag_block.shape[0], ("row", "col")),
        place_of(order, upper_in.shape[0], "row"),
        in_col_order[None, :],
    )
    block_rows = rows // block_mask.shape[1]
    flags = block_mask[0].astype(jnp.float32)
    flags = jnp.repeat(flags, block_rows, axis=0)
    flags = jnp.where(parity == 0, flags[:, ::-1], flags)
    def columns_of(place, first, last):
        return lax.dynamic_slice_in_dim(upper_in, place * half + first, last - first, 1)

    cut = raw_end + EARLY * width
    early = doubled(columns_of(1 - parity, 0, cut), "row", 0)
    late = after(columns_of(1 - parity, cut, half), panel)
    late = next_doubled(late, "row", 0, 0)

    hi, lo, plain_left, sent_left, kept_left = factor(whole_block, orders, panel, flags)

    left_share = lax.dynamic_slice_in_dim(plain_left, col * lower_in.shape[1], lower_in.shape[1], 1)
    left_received = partner(left_share, "cube", 1)
    share = upper_in.shape[0]
    share_hi = lax.dynamic_slice_in_dim(hi, row * share, share, 0)
    share_lo = lax.dynamic_slice_in_dim(lo, row * share, share, 0)
    col_order = index_at(every, lower_in.shape[1], "col")
    row_order = index_at(every, upper_in.shape[0], "row")
    same = (after(col_order, hi)[:, None] == row_order[None, :]).astype(jnp.bfloat16)

    def choice(order):
        return (order[:, None] == jnp.arange(rows, dtype=jnp.int32)[None, :]).astype(jnp.bfloat16)

    chosen = choice(after(row_map[0], hi))

    bounds = [width * unit for unit in PARTS]
    bounds.insert(-1, half - raw_width)
    if raw_width == width:
        bounds = [width * unit for unit in EVEN_PARTS]
    spans = list(zip(bounds, bounds[1:]))
    sent, received = [], []
    merged = None

    def merge(number):
        start, end = spans[number]
        return merge_chunk(
            kept_place, hi, lo, kept_left, trailing, chosen, received[number], [kept_upper], [0], start, end,
            min(width, end - start), merged,
        )

    for number, (start, end) in enumerate(spans):
        before = []
        if number >= AHEAD - 1:
            before += [(raw_received[1:] + received)[number - AHEAD + 1], sent[-1]]
        if number == 1:
            for step in range(1, len(bits_of("row"))):
                late = next_doubled(after(late, sent[0]), "row", 0, step)
        if number == 3:
            before += [left_received]
        if number == 4:
            kept_upper = next_doubled(after(columns_of(parity, 0, half), received[0], sent[3]), "row", 0, 0)
            before += [kept_upper]
        if number == 5:
            for step in range(1, len(bits_of("row"))):
                kept_upper = next_doubled(after(kept_upper, received[1], sent[4]), "row", 0, step)
            raw_upper = after(early[:, :raw_end], received[1], sent[4])
            right_share = (fast(share_hi, raw_upper) + fast(share_lo, raw_upper)).astype(jnp.bfloat16)
            right_received = partner(right_share, "cube", 1)
            before += [kept_upper]
        if number == 6:
            other_left = doubled(after(left_received, received[2], sent[5]), "col", 1)
            before += [other_left]
        if number == 7:
            before += [right_received]
        if number == 8:
            other_right = doubled(after(right_received, received[4], sent[7]), "row", 0)
            other_flags = after(other_small[rows:], received[4]).reshape(block_mask.shape[1:]).astype(jnp.float32)
            other_flags = jnp.where(parity == 0, other_flags[:, :1], other_flags[:, 1:])
            other_left = fast(other_left, same) * jnp.repeat(other_flags, block_rows, axis=0)
            other_left = other_left.astype(jnp.bfloat16)
            other_chosen = choice(after(other_small[:rows], received[4]))
            before += [other_left, other_right, other_chosen]
        for ready in MERGES.get(number, ()):
            merged = merge(ready)
            before += [merged]
        place = after(sent_place, *before) if before else sent_place
        piece, first = (early, 0) if end <= cut else (late, cut)
        sent.append(
            send_chunk(
                place, hi, lo, sent_left, trailing, [piece], [first], start, end, min(width, end - start)
            )
        )
        outgoing = sent[-1]
        if number == len(spans) - 1:
            outgoing = fast(other_chosen, outgoing).astype(jnp.bfloat16)
        received.append(partner(outgoing, "cube", 1))

    for (first, last), arrived in zip(zip(raw_bounds, raw_bounds[1:]), raw_received):
        merged = merge_chunk(
            kept_place, hi, lo, kept_left, trailing, chosen, arrived, [kept_upper], [0], first, last, raw_width,
            merged, (other_left, other_right),
        )
    for number in range(1 + max(map(max, MERGES.values())), len(spans) - 1):
        merged = merge(number)
    start, end = spans[-1]
    own = send_chunk(
        after(kept_place, merged), hi, lo, kept_left, trailing, [kept_upper], [0], start, end, end - start
    )
    merged = join_chunk(own, received[-1], start, merged)
    return merged[None]


def solution(mesh):
    return jax.shard_map(
        local,
        mesh=mesh,
        in_specs=(
            P("cube", ("row", "col"), None),
            P("cube", None),
            P("cube", "row", "col"),
            P("cube", "row", "col"),
            P("cube", "row", "col"),
            P("cube", "row", "col"),
            P("cube", "row"),
        ),
        out_specs=P("cube", "row", "col"),
        check_vma=False,
    )
```

```python
import functools

import jax
import jax.numpy as jnp
from jax import lax
from jax.experimental import pallas as pl
from jax.experimental.pallas import tpu as pltpu
from jax.sharding import PartitionSpec as P

CHUNKS = 15
RAW = 2
EARLY = 2
AHEAD = 3
MERGES = {6: (0,), 7: (1,), 8: (2, 3), 9: (4,), 10: ("raw",), 11: (5, 6), 12: (7, 8)}
ROW_STEPS = 4
HIGH = lax.Precision.HIGHEST
VMEM_LIMIT = 48 * 1024 * 1024


def partner(block, axis, bits):
    count = lax.axis_size(axis)
    return lax.ppermute(block, axis, [(i, i ^ bits) for i in range(count)])


def exact(left, right):
    return jnp.dot(left, right, precision=HIGH, preferred_element_type=jnp.float32)


def fast(left, right):
    return jnp.dot(left, right, preferred_element_type=jnp.float32)


def split(value):
    high = value.astype(jnp.bfloat16)
    return high, (value - high.astype(jnp.float32)).astype(jnp.bfloat16)


def eliminate(block):
    size = block.shape[0]
    row = lax.broadcasted_iota(jnp.int32, (size, size), 0)
    lane = lax.broadcasted_iota(jnp.int32, (size, size), 1)

    def eight(turn, work):
        left = size - 8 * turn
        for step in range(8):
            column = work[:, step : step + 1]
            pivot_row = work[step : step + 1, :]
            inverse = 1.0 / work[step : step + 1, step : step + 1]
            scaled = pivot_row * inverse
            lane_one = lane[:1]
            at = lane_one == step
            passed = (lane_one < step) | (lane_one >= left)
            for_later = jnp.where(at, inverse, scaled)
            for_passed = jnp.where(passed | at, 0.0, scaled)
            row_passed = (row < step) | (row >= left)
            base = jnp.where((lane == step) & jnp.logical_not(row_passed), 0.0, work)
            fresh = base - column * jnp.where(row_passed, for_passed, for_later)
            own = jnp.where(at, inverse, jnp.where(passed, pivot_row, -scaled))
            work = jnp.where(row == step, own, fresh)
        work = jnp.concatenate([work[8:], work[:8]], axis=0)
        return pltpu.roll(work, size - 8, 1)

    return lax.fori_loop(0, size // 8, eight, block)


def inverses(block):
    size = block.shape[0]
    work = eliminate(block)
    row = lax.broadcasted_iota(jnp.int32, (size, size), 0)
    lane = lax.broadcasted_iota(jnp.int32, (size, size), 1)
    diagonal = jnp.sum(jnp.where(row == lane, work, 0.0), axis=0, keepdims=True)
    lower = jnp.where(row > lane, work, jnp.where(row == lane, 1.0, 0.0))
    upper = jnp.where(row < lane, work * diagonal, jnp.where(row == lane, work, 0.0))
    return lower, upper


def factor_kernel(
    block, order_of_diag, order_of_upper, order, order_of_lower, panel, mask, hi, lo, kept_hi, kept_lo, plain, sent, kept
):
    size = block.shape[0]
    half = size // 2
    lane = lax.broadcasted_iota(jnp.int32, (size, size), 1)

    def chosen(order):
        return jnp.where(order[...] == lane, 1.0, 0.0)

    pivoted = exact(chosen(order_of_diag), block[...])
    lower_one, upper_one = inverses(pivoted[:half, :half])
    lower_side = exact(pivoted[half:, :half], upper_one)
    upper_side = exact(lower_one, pivoted[:half, half:])
    schur = pivoted[half:, half:] - exact(lower_side, upper_side)
    lower_two, upper_two = inverses(schur)
    zero = jnp.zeros((half, half), jnp.float32)
    corner_lower = -exact(lower_two, exact(lower_side, lower_one))
    corner_upper = -exact(upper_one, exact(upper_side, upper_two))
    lower_inv = jnp.concatenate(
        [jnp.concatenate([lower_one, zero], 1), jnp.concatenate([corner_lower, lower_two], 1)], 0
    )
    upper_inv = jnp.concatenate(
        [jnp.concatenate([upper_one, corner_upper], 1), jnp.concatenate([zero, upper_two], 1)], 0
    )
    hi[...], lo[...] = split(exact(lower_inv, chosen(order_of_upper)))
    kept_hi[...], kept_lo[...] = split(exact(lower_inv, chosen(order)))
    row = lax.broadcasted_iota(jnp.int32, (size, size), 0)
    in_order = jnp.where(order_of_lower[...] == row, 1.0, 0.0)
    upper_hi, upper_lo = split(exact(in_order, upper_inv))
    for start in range(0, panel.shape[0], size):
        rows = slice(start, start + size)
        part = panel[rows, :]
        result = fast(part, upper_hi) + fast(part, upper_lo)
        plain[rows, :] = result.astype(jnp.bfloat16)
        result = result.astype(jnp.bfloat16).astype(jnp.float32)
        sent[rows, :] = (result * mask[rows, 0:1]).astype(jnp.bfloat16)
        kept[rows, :] = (result * mask[rows, 1:2]).astype(jnp.bfloat16)


def factor(block, orders, panel, mask):
    size = block.shape[0]
    rows = panel.shape[0]
    half_type = jnp.bfloat16
    return pl.pallas_call(
        factor_kernel,
        out_shape=(
            jax.ShapeDtypeStruct((size, size), half_type),
            jax.ShapeDtypeStruct((size, size), half_type),
            jax.ShapeDtypeStruct((size, size), half_type),
            jax.ShapeDtypeStruct((size, size), half_type),
            jax.ShapeDtypeStruct((rows, size), half_type),
            jax.ShapeDtypeStruct((rows, size), half_type),
            jax.ShapeDtypeStruct((rows, size), half_type),
        ),
        compiler_params=pltpu.CompilerParams(vmem_limit_bytes=VMEM_LIMIT),
        cost_estimate=pl.CostEstimate(flops=30_000_000_000, bytes_accessed=3_000_000, transcendentals=0),
        name="factor",
    )(block, *orders, panel, mask)


def panel_tile(hi, lo, pieces):
    columns = jnp.concatenate([piece[...] for piece in pieces], axis=0)
    return (fast(hi[...], columns) + fast(lo[...], columns)).astype(jnp.bfloat16)


def copy_kernel(place, source, out):
    out[...] = source[...]


def take_raw(place, trailing, end):
    rows, columns = trailing.shape
    step_rows = rows // 8
    half_blocks = columns // 2 // end
    if columns // 2 % end:
        return lax.dynamic_slice_in_dim(trailing, place[0] * (columns // 2), end, 1)
    return pl.pallas_call(
        copy_kernel,
        grid_spec=pltpu.PrefetchScalarGridSpec(
            num_scalar_prefetch=1,
            grid=(8,),
            in_specs=[pl.BlockSpec((step_rows, end), lambda i, place: (i, place[0] * half_blocks))],
            out_specs=pl.BlockSpec((step_rows, end), lambda i, place: (i, 0)),
        ),
        out_shape=jax.ShapeDtypeStruct((rows, end), trailing.dtype),
        compiler_params=pltpu.CompilerParams(vmem_limit_bytes=VMEM_LIMIT),
        cost_estimate=pl.CostEstimate(flops=0, bytes_accessed=4 * rows * end, transcendentals=0),
        name="raw_part",
    )(place, trailing)


def send_kernel(place, hi, lo, left, trailing, *rest):
    *pieces, out, right = rest

    @pl.when(pl.program_id(0) == 0)
    def _():
        right[...] = panel_tile(hi, lo, pieces)

    out[...] = (trailing[...].astype(jnp.float32) - fast(left[...], right[...])).astype(jnp.bfloat16)


def merge_kernel(place, hi, lo, left, trailing, chosen, received, *rest):
    *pieces, out, right = rest

    @pl.when(pl.program_id(0) == 0)
    def _():
        right[...] = panel_tile(hi, lo, pieces)

    own = (trailing[...].astype(jnp.float32) - fast(left[...], right[...])).astype(jnp.bfloat16)
    out[...] = (own.astype(jnp.float32) + fast(chosen[...], received[...])).astype(jnp.bfloat16)


def merge_kernel_into(place, hi, lo, left, trailing, chosen, received, *rest):
    *pieces, _, out, right = rest
    merge_kernel(place, hi, lo, left, trailing, chosen, received, *pieces, out, right)


def merge_raw_kernel(place, hi, lo, left, trailing, chosen, received, other_left, other_right, *rest):
    *pieces, out, right, updated = rest

    @pl.when(pl.program_id(0) == 0)
    def _():
        size = out.shape[0]
        for first in range(0, received.shape[0], size):
            rows = slice(first, first + size)
            update = fast(other_left[rows, :], other_right[...])
            updated[rows, :] = (received[rows, :].astype(jnp.float32) - update).astype(jnp.bfloat16)

    merge_kernel(place, hi, lo, left, trailing, chosen, updated, *pieces, out, right)


def merge_raw_kernel_into(*refs):
    merge_raw_kernel(*refs[:-4], *refs[-3:])


def specs_for(hi, left, columns, width, start, pieces, starts):
    size = hi.shape[0]
    rows = left.shape[0] // ROW_STEPS
    half_blocks, chunk = columns // 2 // width, start // width
    whole = pl.BlockSpec((size, size), lambda i, place: (0, 0))
    specs = [
        whole,
        whole,
        pl.BlockSpec((rows, size), lambda i, place: (i, 0)),
        pl.BlockSpec((rows, width), lambda i, place: (i, place[0] * half_blocks + chunk)),
    ]
    piece_specs = []
    for piece, first in zip(pieces, starts):
        block = (piece.shape[0], width)
        if first is None:
            piece_specs.append(pl.BlockSpec(block, lambda i, place: (0, place[0] * half_blocks + chunk)))
        else:
            piece_specs.append(pl.BlockSpec(block, lambda i, place, at=(start - first) // width: (0, at)))
    return specs, piece_specs


def send_chunk(place, hi, lo, left, trailing, pieces, starts, start, width):
    rows, columns = trailing.shape
    specs, piece_specs = specs_for(hi, left, columns, width, start, pieces, starts)
    return pl.pallas_call(
        send_kernel,
        grid_spec=pltpu.PrefetchScalarGridSpec(
            num_scalar_prefetch=1,
            grid=(ROW_STEPS,),
            in_specs=specs + piece_specs,
            out_specs=pl.BlockSpec((rows // ROW_STEPS, width), lambda i, place: (i, 0)),
            scratch_shapes=[pltpu.VMEM((hi.shape[0], width), jnp.bfloat16)],
        ),
        out_shape=jax.ShapeDtypeStruct((rows, width), jnp.bfloat16),
        compiler_params=pltpu.CompilerParams(vmem_limit_bytes=VMEM_LIMIT),
        cost_estimate=pl.CostEstimate(flops=2 * rows * 256 * width, bytes_accessed=5 * rows * width, transcendentals=0),
        name="send_part",
    )(place, hi, lo, left, trailing, *pieces)


def merge_chunk(place, hi, lo, left, trailing, chosen, received, pieces, starts, start, width, merged, raw=None):
    rows, columns = trailing.shape
    step_rows = rows // ROW_STEPS
    specs, piece_specs = specs_for(hi, left, columns, width, start, pieces, starts)
    specs.append(pl.BlockSpec((step_rows, rows), lambda i, place: (i, 0)))
    operands = [place, hi, lo, left, trailing, chosen, received]
    scratch = [pltpu.VMEM((hi.shape[0], width), jnp.bfloat16)]
    body, body_into = merge_kernel, merge_kernel_into
    if raw is None:
        specs.append(pl.BlockSpec((rows, width), lambda i, place: (0, 0)))
    else:
        first, other_left, other_right = raw
        at = (start - first) // width
        specs.append(pl.BlockSpec((rows, width), lambda i, place: (0, at)))
        specs.append(pl.BlockSpec(other_left.shape, lambda i, place: (0, 0)))
        specs.append(pl.BlockSpec((other_right.shape[0], width), lambda i, place: (0, at)))
        operands += [other_left, other_right]
        scratch.append(pltpu.VMEM((rows, width), jnp.bfloat16))
        body, body_into = merge_raw_kernel, merge_raw_kernel_into
    specs += piece_specs
    operands += pieces
    aliases = {}
    if merged is not None:
        aliases = {len(operands): 0}
        operands.append(merged)
        specs.append(pl.BlockSpec(memory_space=pl.ANY))
        body = body_into
    chunk = start // width
    return pl.pallas_call(
        body,
        grid_spec=pltpu.PrefetchScalarGridSpec(
            num_scalar_prefetch=1,
            grid=(ROW_STEPS,),
            in_specs=specs,
            out_specs=pl.BlockSpec((step_rows, width), lambda i, place: (i, chunk)),
            scratch_shapes=scratch,
        ),
        out_shape=jax.ShapeDtypeStruct((rows, columns // 2), jnp.bfloat16),
        input_output_aliases=aliases,
        compiler_params=pltpu.CompilerParams(vmem_limit_bytes=VMEM_LIMIT),
        cost_estimate=pl.CostEstimate(flops=2 * rows * (rows + 256) * width, bytes_accessed=8 * rows * width, transcendentals=0),
        name="merge_part",
    )(*operands)


def join_kernel(own, received, _, out):
    out[...] = (own[...].astype(jnp.float32) + received[...].astype(jnp.float32)).astype(jnp.bfloat16)


def join_chunk(own, received, start, merged):
    rows, width = own.shape
    step_rows = rows // 2
    part = pl.BlockSpec((step_rows, width), lambda i: (i, 0))
    return pl.pallas_call(
        join_kernel,
        grid=(2,),
        in_specs=[part, part, pl.BlockSpec(memory_space=pl.ANY)],
        out_specs=pl.BlockSpec((step_rows, width), lambda i: (i, start // width)),
        out_shape=jax.ShapeDtypeStruct(merged.shape, merged.dtype),
        input_output_aliases={2: 0},
        compiler_params=pltpu.CompilerParams(vmem_limit_bytes=VMEM_LIMIT),
        cost_estimate=pl.CostEstimate(flops=rows * width, bytes_accessed=6 * rows * width, transcendentals=0),
        name="join_part",
    )(own, received, merged)


def bits_of(axis):
    bits = [1 << bit for bit in reversed(range((lax.axis_size(axis) - 1).bit_length()))]
    if not isinstance(axis, str):
        last = lax.axis_size(axis[1:])
        bits = [bit for bit in bits if bit != last] + [last]
    return bits


def doubled(block, axis, dimension):
    for step in range(len(bits_of(axis))):
        block = next_doubled(block, axis, dimension, step)
    return block


def next_doubled(block, axis, dimension, step):
    return jnp.concatenate([block, partner(block, axis, bits_of(axis)[step])], axis=dimension)


def place_of(index, part, axis):
    apart = (index // part) ^ lax.axis_index(axis)
    place = jnp.zeros_like(index)
    for number, bits in enumerate(bits_of(axis)):
        place = place + jnp.where(apart & bits != 0, 1 << number, 0)
    return place * part + index % part


def after(value, *others):
    return lax.optimization_barrier((value, *others))[0]


def local(diag_block, pivot_order, lower_in, upper_in, trailing, block_mask, row_map):
    diag_block, lower_in, upper_in, trailing = diag_block[0], lower_in[0], upper_in[0], trailing[0]
    size = diag_block.shape[1]
    rows, columns = trailing.shape
    half = columns // 2
    width = half // CHUNKS
    row, col = lax.axis_index("row"), lax.axis_index("col")
    parity = lax.axis_index("cube") % 2
    sent_place = (1 - parity).astype(jnp.int32).reshape(1)
    kept_place = parity.astype(jnp.int32).reshape(1)
    raw_end = RAW * width

    raw = take_raw(sent_place, trailing, raw_end)
    raw_received = partner(raw, "cube", 1)

    whole_block = doubled(after(diag_block, raw), ("row", "col"), 0)
    panel = doubled(lower_in, "col", 1)
    order = pivot_order[0][:, None]
    every = jnp.arange(size, dtype=jnp.int32)
    in_col_order = place_of(every, lower_in.shape[1], "col")
    orders = (
        place_of(order, diag_block.shape[0], ("row", "col")),
        place_of(order, upper_in.shape[0], "row"),
        order,
        in_col_order[None, :],
    )
    block_rows = rows // block_mask.shape[1]
    flags = block_mask[0].astype(jnp.float32)
    flags = jnp.repeat(jnp.where(parity == 0, flags[:, ::-1], flags), block_rows, axis=0)
    def columns_of(place, first, last):
        return lax.dynamic_slice_in_dim(upper_in, place * half + first, last - first, 1)

    cut = raw_end + EARLY * width
    early = doubled(columns_of(1 - parity, 0, cut), "row", 0)
    late = columns_of(1 - parity, cut, half)
    late = next_doubled(late, "row", 0, 0)

    hi, lo, kept_hi, kept_lo, plain_left, sent_left, kept_left = factor(whole_block, orders, panel, flags)

    left_share = lax.dynamic_slice_in_dim(plain_left, col * lower_in.shape[1], lower_in.shape[1], 1)
    share = upper_in.shape[0]
    share_hi = lax.dynamic_slice_in_dim(hi, row * share, share, 0)
    share_lo = lax.dynamic_slice_in_dim(lo, row * share, share, 0)
    raw_upper = early[:, :raw_end]
    right_share = (fast(share_hi, raw_upper) + fast(share_lo, raw_upper)).astype(jnp.bfloat16)
    wide = left_share.shape[1]
    stacked = [right_share[:, at : at + wide] for at in range(0, raw_end, wide)]
    mask = block_mask[0].reshape(-1)
    digits = jnp.concatenate([row_map[0] // 32, row_map[0] % 32, mask, jnp.zeros(16 * wide - mask.shape[0], mask.dtype)])
    bundle = jnp.concatenate([left_share, *stacked, digits.astype(jnp.bfloat16).reshape(-1, wide)], axis=0)
    bundle = partner(bundle, "cube", 1)
    def choice(order):
        return (order[:, None] == jnp.arange(rows, dtype=jnp.int32)[None, :]).astype(jnp.bfloat16)

    chosen = choice(after(row_map[0], hi))

    bounds = [width * chunk for chunk in range(RAW, CHUNKS + 1)]
    if width % 256 == 0:
        bounds.insert(-1, half - width // 2)
    spans = list(zip(bounds, bounds[1:]))
    sent, received, merged_after = [], [], []
    merged = None

    def merge(number):
        start, end = spans[number]
        return merge_chunk(
            kept_place, kept_hi, kept_lo, kept_left, trailing, chosen, received[number], [kept_upper], [0], start, end - start,
            merged,
        )

    def merge_raw():
        result = merged
        for start in range(0, raw_end, width):
            result = merge_chunk(
                kept_place, kept_hi, kept_lo, kept_left, trailing, chosen, raw_received, [kept_upper], [0], start,
                width, result, (0, other_left, other_right),
            )
        return result

    for number, (start, end) in enumerate(spans):
        before = []
        if number >= AHEAD - 1:
            before += [([raw_received] + received)[number - AHEAD + 1], sent[-1]]
        if number == 1:
            for step in range(1, len(bits_of("row"))):
                late = next_doubled(after(late, sent[0]), "row", 0, step)
        if number == 2:
            before += [bundle]
        if number == 3:
            kept_upper = after(columns_of(parity, 0, half), received[0], sent[2])
            kept_upper = lax.all_gather(kept_upper, "row", axis=0, tiled=True)
        if number == 5:
            arrived = after(bundle, received[2], sent[4])
            left_received = arrived[:rows]
            stacked = arrived[rows : rows + share * (raw_end // wide)].reshape(raw_end // wide, share, wide)
            right_received = jnp.concatenate(list(stacked), axis=1)
            digits = arrived[rows + share * (raw_end // wide) :].reshape(-1).astype(jnp.float32)
            other_order = (32 * digits[:rows] + digits[rows : 2 * rows]).astype(jnp.int32)
            other_flags = digits[2 * rows : 2 * rows + mask.shape[0]].reshape(block_mask.shape[1:])
            other_flags = jnp.where(parity == 0, other_flags[:, :1], other_flags[:, 1:])
            other_chosen = choice(other_order)
            other_left = lax.all_gather(left_received, "col", axis=1, tiled=True)
            other_left = other_left.astype(jnp.float32) * jnp.repeat(other_flags, block_rows, axis=0)
            other_left = other_left.astype(jnp.bfloat16)
        if number == 6:
            before += [kept_upper]
        if number == 7:
            other_right = lax.all_gather(after(right_received, received[4], sent[6]), "row", axis=0, tiled=True)
        if number == 9:
            before += [other_left, other_right, other_chosen]
        ready = MERGES.get(number, ())
        for item in ready:
            merged = merge_raw() if item == "raw" else merge(item)
        if ready:
            before += [merged]
        place = after(sent_place, *before) if before else sent_place
        piece, first = (early, 0) if end <= cut else (late, cut)
        sent.append(send_chunk(place, hi, lo, sent_left, trailing, [piece], [first], start, end - start))
        outgoing = sent[-1]
        if number == len(spans) - 1:
            outgoing = fast(other_chosen, outgoing).astype(jnp.bfloat16)
        received.append(partner(outgoing, "cube", 1))

    for number in range(1 + MERGES[max(MERGES)][-1], len(spans) - 1):
        merged = merge(number)
    start, end = spans[-1]
    own = send_chunk(
        after(kept_place, merged), kept_hi, kept_lo, kept_left, trailing, [kept_upper], [0], start, end - start
    )
    merged = join_chunk(own, received[-1], start, merged)
    return merged[None]


def solution(mesh):
    return jax.shard_map(
        local,
        mesh=mesh,
        in_specs=(
            P("cube", ("row", "col"), None),
            P("cube", None),
            P("cube", "row", "col"),
            P("cube", "row", "col"),
            P("cube", "row", "col"),
            P("cube", "row", "col"),
            P("cube", "row"),
        ),
        out_specs=P("cube", "row", "col"),
        check_vma=False,
    )
```

```python
import functools

import jax
import jax.numpy as jnp
from jax import lax
from jax.experimental import pallas as pl
from jax.experimental.pallas import tpu as pltpu
from jax.sharding import PartitionSpec as P

CHUNKS = 15
RAW = 2
EARLY = 2
AHEAD = 3
MERGES = {6: (0,), 7: (1,), 8: (2, 3), 9: (4,), 10: ("raw",), 11: (5, 6), 12: (7, 8)}
ROW_STEPS = 4
HIGH = lax.Precision.HIGHEST
VMEM_LIMIT = 48 * 1024 * 1024


def partner(block, axis, bits):
    count = lax.axis_size(axis)
    return lax.ppermute(block, axis, [(i, i ^ bits) for i in range(count)])


def exact(left, right):
    return jnp.dot(left, right, precision=HIGH, preferred_element_type=jnp.float32)


def fast(left, right):
    return jnp.dot(left, right, preferred_element_type=jnp.float32)


def split(value):
    high = value.astype(jnp.bfloat16)
    return high, (value - high.astype(jnp.float32)).astype(jnp.bfloat16)


def eliminate(block):
    size = block.shape[0]
    row = lax.broadcasted_iota(jnp.int32, (size, size), 0)
    lane = lax.broadcasted_iota(jnp.int32, (size, size), 1)

    def eight(turn, work):
        left = size - 8 * turn
        for step in range(8):
            column = work[:, step : step + 1]
            pivot_row = work[step : step + 1, :]
            inverse = 1.0 / work[step : step + 1, step : step + 1]
            scaled = pivot_row * inverse
            lane_one = lane[:1]
            at = lane_one == step
            passed = (lane_one < step) | (lane_one >= left)
            for_later = jnp.where(at, inverse, scaled)
            for_passed = jnp.where(passed | at, 0.0, scaled)
            row_passed = (row < step) | (row >= left)
            base = jnp.where((lane == step) & jnp.logical_not(row_passed), 0.0, work)
            fresh = base - column * jnp.where(row_passed, for_passed, for_later)
            own = jnp.where(at, inverse, jnp.where(passed, pivot_row, -scaled))
            work = jnp.where(row == step, own, fresh)
        work = jnp.concatenate([work[8:], work[:8]], axis=0)
        return pltpu.roll(work, size - 8, 1)

    return lax.fori_loop(0, size // 8, eight, block)


def inverses(block):
    size = block.shape[0]
    work = eliminate(block)
    row = lax.broadcasted_iota(jnp.int32, (size, size), 0)
    lane = lax.broadcasted_iota(jnp.int32, (size, size), 1)
    diagonal = jnp.sum(jnp.where(row == lane, work, 0.0), axis=0, keepdims=True)
    lower = jnp.where(row > lane, work, jnp.where(row == lane, 1.0, 0.0))
    upper = jnp.where(row < lane, work * diagonal, jnp.where(row == lane, work, 0.0))
    return lower, upper


def factor_kernel(
    block, order_of_diag, order_of_upper, order_of_lower, panel, mask, hi, lo, plain, sent, kept
):
    size = block.shape[0]
    half = size // 2
    lane = lax.broadcasted_iota(jnp.int32, (size, size), 1)

    def chosen(order):
        return jnp.where(order[...] == lane, 1.0, 0.0)

    pivoted = exact(chosen(order_of_diag), block[...])
    lower_one, upper_one = inverses(pivoted[:half, :half])
    lower_side = exact(pivoted[half:, :half], upper_one)
    upper_side = exact(lower_one, pivoted[:half, half:])
    schur = pivoted[half:, half:] - exact(lower_side, upper_side)
    lower_two, upper_two = inverses(schur)
    zero = jnp.zeros((half, half), jnp.float32)
    corner_lower = -exact(lower_two, exact(lower_side, lower_one))
    corner_upper = -exact(upper_one, exact(upper_side, upper_two))
    lower_inv = jnp.concatenate(
        [jnp.concatenate([lower_one, zero], 1), jnp.concatenate([corner_lower, lower_two], 1)], 0
    )
    upper_inv = jnp.concatenate(
        [jnp.concatenate([upper_one, corner_upper], 1), jnp.concatenate([zero, upper_two], 1)], 0
    )
    hi[...], lo[...] = split(exact(lower_inv, chosen(order_of_upper)))
    row = lax.broadcasted_iota(jnp.int32, (size, size), 0)
    in_order = jnp.where(order_of_lower[...] == row, 1.0, 0.0)
    upper_hi, upper_lo = split(exact(in_order, upper_inv))
    for start in range(0, panel.shape[0], size):
        rows = slice(start, start + size)
        part = panel[rows, :]
        result = fast(part, upper_hi) + fast(part, upper_lo)
        plain[rows, :] = result.astype(jnp.bfloat16)
        result = result.astype(jnp.bfloat16).astype(jnp.float32)
        sent[rows, :] = (result * mask[rows, 0:1]).astype(jnp.bfloat16)
        kept[rows, :] = (result * mask[rows, 1:2]).astype(jnp.bfloat16)


def factor(block, orders, panel, mask):
    size = block.shape[0]
    rows = panel.shape[0]
    half_type = jnp.bfloat16
    return pl.pallas_call(
        factor_kernel,
        out_shape=(
            jax.ShapeDtypeStruct((size, size), half_type),
            jax.ShapeDtypeStruct((size, size), half_type),
            jax.ShapeDtypeStruct((rows, size), half_type),
            jax.ShapeDtypeStruct((rows, size), half_type),
            jax.ShapeDtypeStruct((rows, size), half_type),
        ),
        compiler_params=pltpu.CompilerParams(vmem_limit_bytes=VMEM_LIMIT),
        cost_estimate=pl.CostEstimate(flops=30_000_000_000, bytes_accessed=3_000_000, transcendentals=0),
        name="factor",
    )(block, *orders, panel, mask)


def panel_tile(hi, lo, pieces):
    columns = jnp.concatenate([piece[...] for piece in pieces], axis=0)
    return (fast(hi[...], columns) + fast(lo[...], columns)).astype(jnp.bfloat16)


def copy_kernel(place, source, out):
    out[...] = source[...]


def take_raw(place, trailing, end):
    rows, columns = trailing.shape
    step_rows = rows // 8
    half_blocks = columns // 2 // end
    if columns // 2 % end:
        return lax.dynamic_slice_in_dim(trailing, place[0] * (columns // 2), end, 1)
    return pl.pallas_call(
        copy_kernel,
        grid_spec=pltpu.PrefetchScalarGridSpec(
            num_scalar_prefetch=1,
            grid=(8,),
            in_specs=[pl.BlockSpec((step_rows, end), lambda i, place: (i, place[0] * half_blocks))],
            out_specs=pl.BlockSpec((step_rows, end), lambda i, place: (i, 0)),
        ),
        out_shape=jax.ShapeDtypeStruct((rows, end), trailing.dtype),
        compiler_params=pltpu.CompilerParams(vmem_limit_bytes=VMEM_LIMIT),
        cost_estimate=pl.CostEstimate(flops=0, bytes_accessed=4 * rows * end, transcendentals=0),
        name="raw_part",
    )(place, trailing)


def send_kernel(place, hi, lo, left, trailing, *rest):
    *pieces, out, right = rest

    @pl.when(pl.program_id(0) == 0)
    def _():
        right[...] = panel_tile(hi, lo, pieces)

    out[...] = (trailing[...].astype(jnp.float32) - fast(left[...], right[...])).astype(jnp.bfloat16)


def merge_kernel(place, hi, lo, left, trailing, chosen, received, *rest):
    *pieces, out, right = rest

    @pl.when(pl.program_id(0) == 0)
    def _():
        right[...] = panel_tile(hi, lo, pieces)

    own = (trailing[...].astype(jnp.float32) - fast(left[...], right[...])).astype(jnp.bfloat16)
    out[...] = (own.astype(jnp.float32) + fast(chosen[...], received[...])).astype(jnp.bfloat16)


def merge_kernel_into(place, hi, lo, left, trailing, chosen, received, *rest):
    *pieces, _, out, right = rest
    merge_kernel(place, hi, lo, left, trailing, chosen, received, *pieces, out, right)


def merge_raw_kernel(place, hi, lo, left, trailing, chosen, received, other_left, other_right, *rest):
    *pieces, out, right, updated = rest

    @pl.when(pl.program_id(0) == 0)
    def _():
        size = out.shape[0]
        for first in range(0, received.shape[0], size):
            rows = slice(first, first + size)
            update = fast(other_left[rows, :], other_right[...])
            updated[rows, :] = (received[rows, :].astype(jnp.float32) - update).astype(jnp.bfloat16)

    merge_kernel(place, hi, lo, left, trailing, chosen, updated, *pieces, out, right)


def merge_raw_kernel_into(*refs):
    merge_raw_kernel(*refs[:-4], *refs[-3:])


def specs_for(hi, left, columns, width, start, pieces, starts):
    size = hi.shape[0]
    rows = left.shape[0] // ROW_STEPS
    half_blocks, chunk = columns // 2 // width, start // width
    whole = pl.BlockSpec((size, size), lambda i, place: (0, 0))
    specs = [
        whole,
        whole,
        pl.BlockSpec((rows, size), lambda i, place: (i, 0)),
        pl.BlockSpec((rows, width), lambda i, place: (i, place[0] * half_blocks + chunk)),
    ]
    piece_specs = []
    for piece, first in zip(pieces, starts):
        block = (piece.shape[0], width)
        if first is None:
            piece_specs.append(pl.BlockSpec(block, lambda i, place: (0, place[0] * half_blocks + chunk)))
        else:
            piece_specs.append(pl.BlockSpec(block, lambda i, place, at=(start - first) // width: (0, at)))
    return specs, piece_specs


def send_chunk(place, hi, lo, left, trailing, pieces, starts, start, width):
    rows, columns = trailing.shape
    specs, piece_specs = specs_for(hi, left, columns, width, start, pieces, starts)
    return pl.pallas_call(
        send_kernel,
        grid_spec=pltpu.PrefetchScalarGridSpec(
            num_scalar_prefetch=1,
            grid=(ROW_STEPS,),
            in_specs=specs + piece_specs,
            out_specs=pl.BlockSpec((rows // ROW_STEPS, width), lambda i, place: (i, 0)),
            scratch_shapes=[pltpu.VMEM((hi.shape[0], width), jnp.bfloat16)],
        ),
        out_shape=jax.ShapeDtypeStruct((rows, width), jnp.bfloat16),
        compiler_params=pltpu.CompilerParams(vmem_limit_bytes=VMEM_LIMIT),
        cost_estimate=pl.CostEstimate(flops=2 * rows * 256 * width, bytes_accessed=5 * rows * width, transcendentals=0),
        name="send_part",
    )(place, hi, lo, left, trailing, *pieces)


def merge_chunk(place, hi, lo, left, trailing, chosen, received, pieces, starts, start, width, merged, raw=None):
    rows, columns = trailing.shape
    step_rows = rows // ROW_STEPS
    specs, piece_specs = specs_for(hi, left, columns, width, start, pieces, starts)
    specs.append(pl.BlockSpec((step_rows, rows), lambda i, place: (i, 0)))
    operands = [place, hi, lo, left, trailing, chosen, received]
    scratch = [pltpu.VMEM((hi.shape[0], width), jnp.bfloat16)]
    body, body_into = merge_kernel, merge_kernel_into
    if raw is None:
        specs.append(pl.BlockSpec((rows, width), lambda i, place: (0, 0)))
    else:
        first, other_left, other_right = raw
        at = (start - first) // width
        specs.append(pl.BlockSpec((rows, width), lambda i, place: (0, at)))
        specs.append(pl.BlockSpec(other_left.shape, lambda i, place: (0, 0)))
        specs.append(pl.BlockSpec((other_right.shape[0], width), lambda i, place: (0, at)))
        operands += [other_left, other_right]
        scratch.append(pltpu.VMEM((rows, width), jnp.bfloat16))
        body, body_into = merge_raw_kernel, merge_raw_kernel_into
    specs += piece_specs
    operands += pieces
    aliases = {}
    if merged is not None:
        aliases = {len(operands): 0}
        operands.append(merged)
        specs.append(pl.BlockSpec(memory_space=pl.ANY))
        body = body_into
    chunk = start // width
    return pl.pallas_call(
        body,
        grid_spec=pltpu.PrefetchScalarGridSpec(
            num_scalar_prefetch=1,
            grid=(ROW_STEPS,),
            in_specs=specs,
            out_specs=pl.BlockSpec((step_rows, width), lambda i, place: (i, chunk)),
            scratch_shapes=scratch,
        ),
        out_shape=jax.ShapeDtypeStruct((rows, columns // 2), jnp.bfloat16),
        input_output_aliases=aliases,
        compiler_params=pltpu.CompilerParams(vmem_limit_bytes=VMEM_LIMIT),
        cost_estimate=pl.CostEstimate(flops=2 * rows * (rows + 256) * width, bytes_accessed=8 * rows * width, transcendentals=0),
        name="merge_part",
    )(*operands)


def join_kernel(own, received, _, out):
    out[...] = (own[...].astype(jnp.float32) + received[...].astype(jnp.float32)).astype(jnp.bfloat16)


def join_chunk(own, received, start, merged):
    rows, width = own.shape
    step_rows = rows // 2
    part = pl.BlockSpec((step_rows, width), lambda i: (i, 0))
    return pl.pallas_call(
        join_kernel,
        grid=(2,),
        in_specs=[part, part, pl.BlockSpec(memory_space=pl.ANY)],
        out_specs=pl.BlockSpec((step_rows, width), lambda i: (i, start // width)),
        out_shape=jax.ShapeDtypeStruct(merged.shape, merged.dtype),
        input_output_aliases={2: 0},
        compiler_params=pltpu.CompilerParams(vmem_limit_bytes=VMEM_LIMIT),
        cost_estimate=pl.CostEstimate(flops=rows * width, bytes_accessed=6 * rows * width, transcendentals=0),
        name="join_part",
    )(own, received, merged)


def bits_of(axis):
    bits = [1 << bit for bit in reversed(range((lax.axis_size(axis) - 1).bit_length()))]
    if not isinstance(axis, str):
        last = lax.axis_size(axis[1:])
        bits = [bit for bit in bits if bit != last] + [last]
    return bits


def doubled(block, axis, dimension):
    for step in range(len(bits_of(axis))):
        block = next_doubled(block, axis, dimension, step)
    return block


def next_doubled(block, axis, dimension, step):
    return jnp.concatenate([block, partner(block, axis, bits_of(axis)[step])], axis=dimension)


def place_of(index, part, axis):
    apart = (index // part) ^ lax.axis_index(axis)
    place = jnp.zeros_like(index)
    for number, bits in enumerate(bits_of(axis)):
        place = place + jnp.where(apart & bits != 0, 1 << number, 0)
    return place * part + index % part


def after(value, *others):
    return lax.optimization_barrier((value, *others))[0]


def local(diag_block, pivot_order, lower_in, upper_in, trailing, block_mask, row_map):
    diag_block, lower_in, upper_in, trailing = diag_block[0], lower_in[0], upper_in[0], trailing[0]
    size = diag_block.shape[1]
    rows, columns = trailing.shape
    half = columns // 2
    width = half // CHUNKS
    row, col = lax.axis_index("row"), lax.axis_index("col")
    parity = lax.axis_index("cube") % 2
    sent_place = (1 - parity).astype(jnp.int32).reshape(1)
    kept_place = parity.astype(jnp.int32).reshape(1)
    raw_end = RAW * width

    raw = take_raw(sent_place, trailing, raw_end)
    raw_received = partner(raw, "cube", 1)

    whole_block = doubled(after(diag_block, raw), ("row", "col"), 0)
    panel = doubled(lower_in, "col", 1)
    order = pivot_order[0][:, None]
    every = jnp.arange(size, dtype=jnp.int32)
    in_col_order = place_of(every, lower_in.shape[1], "col")
    orders = (
        place_of(order, diag_block.shape[0], ("row", "col")),
        place_of(order, upper_in.shape[0], "row"),
        in_col_order[None, :],
    )
    block_rows = rows // block_mask.shape[1]
    flags = block_mask[0].astype(jnp.float32)
    flags = jnp.repeat(jnp.where(parity == 0, flags[:, ::-1], flags), block_rows, axis=0)
    def columns_of(place, first, last):
        return lax.dynamic_slice_in_dim(upper_in, place * half + first, last - first, 1)

    cut = raw_end + EARLY * width
    early = doubled(columns_of(1 - parity, 0, cut), "row", 0)
    late, kept_upper = columns_of(1 - parity, cut, half), columns_of(parity, 0, half)
    rest = partner(jnp.concatenate([late, kept_upper], axis=1), "row", bits_of("row")[0])
    late = jnp.concatenate([late, rest[:, : half - cut]], axis=0)
    kept_upper = jnp.concatenate([kept_upper, rest[:, half - cut :]], axis=0)

    hi, lo, plain_left, sent_left, kept_left = factor(whole_block, orders, panel, flags)

    left_share = lax.dynamic_slice_in_dim(plain_left, col * lower_in.shape[1], lower_in.shape[1], 1)
    share = upper_in.shape[0]
    share_hi = lax.dynamic_slice_in_dim(hi, row * share, share, 0)
    share_lo = lax.dynamic_slice_in_dim(lo, row * share, share, 0)
    left_received = partner(left_share, "cube", 1)
    mask = block_mask[0].reshape(-1)
    mask_rows = -(-(2 * rows + mask.shape[0]) // (16 * raw_end)) * 16
    fill = jnp.zeros(mask_rows * raw_end - 2 * rows - mask.shape[0], mask.dtype)
    digits = jnp.concatenate([row_map[0] // 32, row_map[0] % 32, mask, fill])
    digits = digits.astype(jnp.bfloat16).reshape(mask_rows, raw_end)

    def choice(order):
        return (order[:, None] == jnp.arange(rows, dtype=jnp.int32)[None, :]).astype(jnp.bfloat16)

    chosen = choice(after(row_map[0], hi))

    bounds = [width * chunk for chunk in range(RAW, CHUNKS + 1)]
    if width % 256 == 0:
        bounds.insert(-1, half - width // 2)
    spans = list(zip(bounds, bounds[1:]))
    sent, received, merged_after = [], [], []
    merged = None

    def merge(number):
        start, end = spans[number]
        return merge_chunk(
            kept_place, hi, lo, kept_left, trailing, chosen, received[number], [kept_upper], [0], start, end - start,
            merged,
        )

    def merge_raw():
        result = merged
        for start in range(0, raw_end, width):
            result = merge_chunk(
                kept_place, hi, lo, kept_left, trailing, chosen, raw_received, [kept_upper], [0], start,
                width, result, (0, other_left, other_right),
            )
        return result

    for number, (start, end) in enumerate(spans):
        before = []
        if number >= AHEAD - 1:
            before += [([raw_received] + received)[number - AHEAD + 1], sent[-1]]
        if number == 1:
            for step in range(1, len(bits_of("row"))):
                late = next_doubled(after(late, sent[0]), "row", 0, step)
        if number == 3:
            before += [left_received]
            for step in range(1, len(bits_of("row"))):
                kept_upper = next_doubled(after(kept_upper, raw_received, sent[2]), "row", 0, step)
            raw_upper = after(early[:, :raw_end], received[0], sent[2])
            right_share = (fast(share_hi, raw_upper) + fast(share_lo, raw_upper)).astype(jnp.bfloat16)
            bundle = partner(jnp.concatenate([right_share, digits], axis=0), "cube", 1)
        if number == 5:
            before += [bundle, kept_upper]
        if number == 6:
            arrived = after(bundle, received[3], sent[5])
            right_received = arrived[:share]
            digits = arrived[share:].reshape(-1).astype(jnp.float32)
            other_order = (32 * digits[:rows] + digits[rows : 2 * rows]).astype(jnp.int32)
            other_flags = digits[2 * rows : 2 * rows + mask.shape[0]].reshape(block_mask.shape[1:])
            other_flags = jnp.where(parity == 0, other_flags[:, :1], other_flags[:, 1:])
            other_chosen = choice(other_order)
            left_received = after(left_received, received[3], sent[5])
            other_left = lax.all_gather(left_received, "col", axis=1, tiled=True)
            other_left = other_left.astype(jnp.float32) * jnp.repeat(other_flags, block_rows, axis=0)
            other_left = other_left.astype(jnp.bfloat16)
        if number == 8:
            other_right = lax.all_gather(after(right_received, received[5], sent[7]), "row", axis=0, tiled=True)
        if number == 9:
            before += [other_left, other_right, other_chosen]
        ready = MERGES.get(number, ())
        for item in ready:
            merged = merge_raw() if item == "raw" else merge(item)
        if ready:
            before += [merged]
        place = after(sent_place, *before) if before else sent_place
        piece, first = (early, 0) if end <= cut else (late, cut)
        sent.append(send_chunk(place, hi, lo, sent_left, trailing, [piece], [first], start, end - start))
        outgoing = sent[-1]
        if number == len(spans) - 1:
            outgoing = fast(other_chosen, outgoing).astype(jnp.bfloat16)
        received.append(partner(outgoing, "cube", 1))

    for number in range(1 + MERGES[max(MERGES)][-1], len(spans) - 1):
        merged = merge(number)
    start, end = spans[-1]
    own = send_chunk(
        after(kept_place, merged), hi, lo, kept_left, trailing, [kept_upper], [0], start, end - start
    )
    merged = join_chunk(own, received[-1], start, merged)
    return merged[None]


def solution(mesh):
    return jax.shard_map(
        local,
        mesh=mesh,
        in_specs=(
            P("cube", ("row", "col"), None),
            P("cube", None),
            P("cube", "row", "col"),
            P("cube", "row", "col"),
            P("cube", "row", "col"),
            P("cube", "row", "col"),
            P("cube", "row"),
        ),
        out_specs=P("cube", "row", "col"),
        check_vma=False,
    )
```

```python
import functools

import jax
import jax.numpy as jnp
from jax import lax
from jax.experimental import pallas as pl
from jax.experimental.pallas import tpu as pltpu
from jax.sharding import PartitionSpec as P

CHUNKS = 15
RAW = 2
EARLY = 2
AHEAD = 3
MERGES = {6: (0,), 7: (1,), 8: (2, 3), 9: (4,), 10: ("raw",), 11: (5, 6), 12: (7, 8)}
ROW_STEPS = 4
HIGH = lax.Precision.HIGHEST
VMEM_LIMIT = 48 * 1024 * 1024


def partner(block, axis, bits):
    count = lax.axis_size(axis)
    return lax.ppermute(block, axis, [(i, i ^ bits) for i in range(count)])


def exact(left, right):
    return jnp.dot(left, right, precision=HIGH, preferred_element_type=jnp.float32)


def fast(left, right):
    return jnp.dot(left, right, preferred_element_type=jnp.float32)


def split(value):
    high = value.astype(jnp.bfloat16)
    return high, (value - high.astype(jnp.float32)).astype(jnp.bfloat16)


def eliminate(block):
    size = block.shape[0]
    row = lax.broadcasted_iota(jnp.int32, (size, size), 0)
    lane = lax.broadcasted_iota(jnp.int32, (size, size), 1)

    def eight(turn, work):
        left = size - 8 * turn
        for step in range(8):
            column = work[:, step : step + 1]
            pivot_row = work[step : step + 1, :]
            inverse = 1.0 / work[step : step + 1, step : step + 1]
            scaled = pivot_row * inverse
            lane_one = lane[:1]
            at = lane_one == step
            passed = (lane_one < step) | (lane_one >= left)
            for_later = jnp.where(at, inverse, scaled)
            for_passed = jnp.where(passed | at, 0.0, scaled)
            row_passed = (row < step) | (row >= left)
            base = jnp.where((lane == step) & jnp.logical_not(row_passed), 0.0, work)
            fresh = base - column * jnp.where(row_passed, for_passed, for_later)
            own = jnp.where(at, inverse, jnp.where(passed, pivot_row, -scaled))
            work = jnp.where(row == step, own, fresh)
        work = jnp.concatenate([work[8:], work[:8]], axis=0)
        return pltpu.roll(work, size - 8, 1)

    return lax.fori_loop(0, size // 8, eight, block)


def inverses(block):
    size = block.shape[0]
    work = eliminate(block)
    row = lax.broadcasted_iota(jnp.int32, (size, size), 0)
    lane = lax.broadcasted_iota(jnp.int32, (size, size), 1)
    diagonal = jnp.sum(jnp.where(row == lane, work, 0.0), axis=0, keepdims=True)
    lower = jnp.where(row > lane, work, jnp.where(row == lane, 1.0, 0.0))
    upper = jnp.where(row < lane, work * diagonal, jnp.where(row == lane, work, 0.0))
    return lower, upper


def factor_kernel(
    place, mask, first, second, orders, left_panel, right_panel, hi, lo, plain, sent, kept
):
    size = first.shape[1]
    half = size // 2
    block = jnp.concatenate([first[...], second[...]], axis=0)
    row = lax.broadcasted_iota(jnp.int32, (size, size), 0)

    def chosen(number):
        return jnp.where(orders[number : number + 1, :] == row, 1.0, 0.0)

    pivoted = exact(chosen(0).T, block)
    lower_one, upper_one = inverses(pivoted[:half, :half])
    lower_side = exact(pivoted[half:, :half], upper_one)
    upper_side = exact(lower_one, pivoted[:half, half:])
    schur = pivoted[half:, half:] - exact(lower_side, upper_side)
    lower_two, upper_two = inverses(schur)
    zero = jnp.zeros((half, half), jnp.float32)
    corner_lower = -exact(lower_two, exact(lower_side, lower_one))
    corner_upper = -exact(upper_one, exact(upper_side, upper_two))
    lower_inv = jnp.concatenate(
        [jnp.concatenate([lower_one, zero], 1), jnp.concatenate([corner_lower, lower_two], 1)], 0
    )
    upper_inv = jnp.concatenate(
        [jnp.concatenate([upper_one, corner_upper], 1), jnp.concatenate([zero, upper_two], 1)], 0
    )
    hi[...], lo[...] = split(exact(lower_inv, chosen(1).T))
    upper_hi, upper_lo = split(exact(chosen(2), upper_inv))
    rows = left_panel.shape[0]
    block_rows = rows // mask.shape[0]
    for start in range(0, rows, size):
        part = jnp.concatenate(
            [left_panel[start : start + size, :], right_panel[start : start + size, :]], axis=1
        )
        result = (fast(part, upper_hi) + fast(part, upper_lo)).astype(jnp.bfloat16)
        plain[start : start + size, :] = result
        result = result.astype(jnp.float32)
        for at in range(start, start + size, block_rows):
            piece = result[at - start : at - start + block_rows]
            number = at // block_rows
            sent[at : at + block_rows, :] = (piece * mask[number, place[0]].astype(jnp.float32)).astype(jnp.bfloat16)
            kept[at : at + block_rows, :] = (piece * mask[number, 1 - place[0]].astype(jnp.float32)).astype(jnp.bfloat16)


def factor(place, mask, first, second, orders, left_panel, right_panel):
    size = first.shape[1]
    rows = left_panel.shape[0]
    half_type = jnp.bfloat16
    scalars = pl.BlockSpec(memory_space=pltpu.SMEM)
    arrays = pl.BlockSpec(memory_space=pltpu.VMEM)
    return pl.pallas_call(
        factor_kernel,
        in_specs=[scalars] * 2 + [arrays] * 5,
        out_shape=(
            jax.ShapeDtypeStruct((size, size), half_type),
            jax.ShapeDtypeStruct((size, size), half_type),
            jax.ShapeDtypeStruct((rows, size), half_type),
            jax.ShapeDtypeStruct((rows, size), half_type),
            jax.ShapeDtypeStruct((rows, size), half_type),
        ),
        compiler_params=pltpu.CompilerParams(vmem_limit_bytes=VMEM_LIMIT),
        cost_estimate=pl.CostEstimate(flops=30_000_000_000, bytes_accessed=3_000_000, transcendentals=0),
        name="factor",
    )(place, mask, first, second, orders, left_panel, right_panel)


def panel_tile(hi, lo, pieces):
    columns = jnp.concatenate([piece[...] for piece in pieces], axis=0)
    return (fast(hi[...], columns) + fast(lo[...], columns)).astype(jnp.bfloat16)


def copy_kernel(place, source, out):
    out[...] = source[...]


def take_raw(place, trailing, end, width):
    rows, columns = trailing.shape
    step_rows = rows // 4
    half_blocks = columns // 2 // width
    return pl.pallas_call(
        copy_kernel,
        grid_spec=pltpu.PrefetchScalarGridSpec(
            num_scalar_prefetch=1,
            grid=(4, end // width),
            in_specs=[pl.BlockSpec((step_rows, width), lambda i, j, place: (i, place[0] * half_blocks + j))],
            out_specs=pl.BlockSpec((step_rows, width), lambda i, j, place: (i, j)),
        ),
        out_shape=jax.ShapeDtypeStruct((rows, end), trailing.dtype),
        compiler_params=pltpu.CompilerParams(vmem_limit_bytes=VMEM_LIMIT),
        cost_estimate=pl.CostEstimate(flops=0, bytes_accessed=4 * rows * end, transcendentals=0),
        name="raw_part",
    )(place, trailing)


def send_kernel(place, hi, lo, left, trailing, *rest):
    *pieces, out, right = rest

    @pl.when(pl.program_id(0) == 0)
    def _():
        right[...] = panel_tile(hi, lo, pieces)

    out[...] = (trailing[...].astype(jnp.float32) - fast(left[...], right[...])).astype(jnp.bfloat16)


def merge_kernel(place, hi, lo, left, trailing, chosen, received, *rest):
    *pieces, out, right = rest

    @pl.when(pl.program_id(0) == 0)
    def _():
        right[...] = panel_tile(hi, lo, pieces)

    own = (trailing[...].astype(jnp.float32) - fast(left[...], right[...])).astype(jnp.bfloat16)
    out[...] = (own.astype(jnp.float32) + fast(chosen[...], received[...])).astype(jnp.bfloat16)


def merge_kernel_into(place, hi, lo, left, trailing, chosen, received, *rest):
    *pieces, _, out, right = rest
    merge_kernel(place, hi, lo, left, trailing, chosen, received, *pieces, out, right)


def merge_raw_kernel(place, hi, lo, left, trailing, chosen, received, other_left, other_right, *rest):
    *pieces, out, right, updated = rest

    @pl.when(pl.program_id(0) == 0)
    def _():
        size = out.shape[0]
        for first in range(0, received.shape[0], size):
            rows = slice(first, first + size)
            update = fast(other_left[rows, :], other_right[...])
            updated[rows, :] = (received[rows, :].astype(jnp.float32) - update).astype(jnp.bfloat16)

    merge_kernel(place, hi, lo, left, trailing, chosen, updated, *pieces, out, right)


def merge_raw_kernel_into(*refs):
    merge_raw_kernel(*refs[:-4], *refs[-3:])


def specs_for(hi, left, columns, width, start, pieces, starts):
    size = hi.shape[0]
    rows = left.shape[0] // ROW_STEPS
    half_blocks, chunk = columns // 2 // width, start // width
    whole = pl.BlockSpec((size, size), lambda i, place: (0, 0))
    specs = [
        whole,
        whole,
        pl.BlockSpec((rows, size), lambda i, place: (i, 0)),
        pl.BlockSpec((rows, width), lambda i, place: (i, place[0] * half_blocks + chunk)),
    ]
    piece_specs = []
    for piece, first in zip(pieces, starts):
        block = (piece.shape[0], width)
        if first is None:
            piece_specs.append(pl.BlockSpec(block, lambda i, place: (0, place[0] * half_blocks + chunk)))
        else:
            piece_specs.append(pl.BlockSpec(block, lambda i, place, at=(start - first) // width: (0, at)))
    return specs, piece_specs


def send_chunk(place, hi, lo, left, trailing, pieces, starts, start, width):
    rows, columns = trailing.shape
    specs, piece_specs = specs_for(hi, left, columns, width, start, pieces, starts)
    return pl.pallas_call(
        send_kernel,
        grid_spec=pltpu.PrefetchScalarGridSpec(
            num_scalar_prefetch=1,
            grid=(ROW_STEPS,),
            in_specs=specs + piece_specs,
            out_specs=pl.BlockSpec((rows // ROW_STEPS, width), lambda i, place: (i, 0)),
            scratch_shapes=[pltpu.VMEM((hi.shape[0], width), jnp.bfloat16)],
        ),
        out_shape=jax.ShapeDtypeStruct((rows, width), jnp.bfloat16),
        compiler_params=pltpu.CompilerParams(vmem_limit_bytes=VMEM_LIMIT),
        cost_estimate=pl.CostEstimate(flops=2 * rows * 256 * width, bytes_accessed=5 * rows * width, transcendentals=0),
        name="send_part",
    )(place, hi, lo, left, trailing, *pieces)


def merge_chunk(place, hi, lo, left, trailing, chosen, received, pieces, starts, start, width, merged, raw=None):
    rows, columns = trailing.shape
    step_rows = rows // ROW_STEPS
    specs, piece_specs = specs_for(hi, left, columns, width, start, pieces, starts)
    specs.append(pl.BlockSpec((step_rows, rows), lambda i, place: (i, 0)))
    operands = [place, hi, lo, left, trailing, chosen, received]
    scratch = [pltpu.VMEM((hi.shape[0], width), jnp.bfloat16)]
    body, body_into = merge_kernel, merge_kernel_into
    if raw is None:
        specs.append(pl.BlockSpec((rows, width), lambda i, place: (0, 0)))
    else:
        first, other_left, other_right = raw
        at = (start - first) // width
        specs.append(pl.BlockSpec((rows, width), lambda i, place: (0, at)))
        specs.append(pl.BlockSpec(other_left.shape, lambda i, place: (0, 0)))
        specs.append(pl.BlockSpec((other_right.shape[0], width), lambda i, place: (0, at)))
        operands += [other_left, other_right]
        scratch.append(pltpu.VMEM((rows, width), jnp.bfloat16))
        body, body_into = merge_raw_kernel, merge_raw_kernel_into
    specs += piece_specs
    operands += pieces
    aliases = {}
    if merged is not None:
        aliases = {len(operands): 0}
        operands.append(merged)
        specs.append(pl.BlockSpec(memory_space=pl.ANY))
        body = body_into
    chunk = start // width
    return pl.pallas_call(
        body,
        grid_spec=pltpu.PrefetchScalarGridSpec(
            num_scalar_prefetch=1,
            grid=(ROW_STEPS,),
            in_specs=specs,
            out_specs=pl.BlockSpec((step_rows, width), lambda i, place: (i, chunk)),
            scratch_shapes=scratch,
        ),
        out_shape=jax.ShapeDtypeStruct((rows, columns // 2), jnp.bfloat16),
        input_output_aliases=aliases,
        compiler_params=pltpu.CompilerParams(vmem_limit_bytes=VMEM_LIMIT),
        cost_estimate=pl.CostEstimate(flops=2 * rows * (rows + 256) * width, bytes_accessed=8 * rows * width, transcendentals=0),
        name="merge_part",
    )(*operands)


def join_kernel(own, received, _, out):
    out[...] = (own[...].astype(jnp.float32) + received[...].astype(jnp.float32)).astype(jnp.bfloat16)


def join_chunk(own, received, start, merged):
    rows, width = own.shape
    step_rows = rows // 2
    part = pl.BlockSpec((step_rows, width), lambda i: (i, 0))
    return pl.pallas_call(
        join_kernel,
        grid=(2,),
        in_specs=[part, part, pl.BlockSpec(memory_space=pl.ANY)],
        out_specs=pl.BlockSpec((step_rows, width), lambda i: (i, start // width)),
        out_shape=jax.ShapeDtypeStruct(merged.shape, merged.dtype),
        input_output_aliases={2: 0},
        compiler_params=pltpu.CompilerParams(vmem_limit_bytes=VMEM_LIMIT),
        cost_estimate=pl.CostEstimate(flops=rows * width, bytes_accessed=6 * rows * width, transcendentals=0),
        name="join_part",
    )(own, received, merged)


def bits_of(axis):
    bits = [1 << bit for bit in reversed(range((lax.axis_size(axis) - 1).bit_length()))]
    if not isinstance(axis, str):
        last = lax.axis_size(axis[1:])
        bits = [bit for bit in bits if bit != last] + [last]
    return bits


def doubled(block, axis, dimension):
    for step in range(len(bits_of(axis))):
        block = next_doubled(block, axis, dimension, step)
    return block


def halves(block, axis, dimension):
    steps = len(bits_of(axis))
    for step in range(steps - 1):
        block = next_doubled(block, axis, dimension, step)
    return block, partner(block, axis, bits_of(axis)[steps - 1])


def next_doubled(block, axis, dimension, step):
    return jnp.concatenate([block, partner(block, axis, bits_of(axis)[step])], axis=dimension)


def place_of(index, part, axis):
    apart = (index // part) ^ lax.axis_index(axis)
    place = jnp.zeros_like(index)
    for number, bits in enumerate(bits_of(axis)):
        place = place + jnp.where(apart & bits != 0, 1 << number, 0)
    return place * part + index % part


def after(value, *others):
    return lax.optimization_barrier((value, *others))[0]


def local(diag_block, pivot_order, lower_in, upper_in, trailing, block_mask, row_map):
    diag_block, lower_in, upper_in, trailing = diag_block[0], lower_in[0], upper_in[0], trailing[0]
    size = diag_block.shape[1]
    rows, columns = trailing.shape
    half = columns // 2
    width = half // CHUNKS
    row, col = lax.axis_index("row"), lax.axis_index("col")
    parity = lax.axis_index("cube") % 2
    sent_place = (1 - parity).astype(jnp.int32).reshape(1)
    kept_place = parity.astype(jnp.int32).reshape(1)
    raw_end = RAW * width

    raw = take_raw(sent_place, trailing, raw_end, width)
    raw_received = partner(raw, "cube", 1)

    diag_halves = halves(after(diag_block, raw), ("row", "col"), 0)
    panel_halves = halves(lower_in, "col", 1)
    order = pivot_order[0]
    every = jnp.arange(size, dtype=jnp.int32)
    orders = jnp.stack([
        place_of(order, diag_block.shape[0], ("row", "col")),
        place_of(order, upper_in.shape[0], "row"),
        place_of(every, lower_in.shape[1], "col"),
    ])
    block_rows = rows // block_mask.shape[1]

    def columns_of(place, first, last):
        return lax.dynamic_slice_in_dim(upper_in, place * half + first, last - first, 1)

    cut = raw_end + EARLY * width
    early = doubled(columns_of(1 - parity, 0, cut), "row", 0)
    late, kept_upper = columns_of(1 - parity, cut, half), columns_of(parity, 0, half)
    rest = partner(jnp.concatenate([late, kept_upper], axis=1), "row", bits_of("row")[0])
    late = jnp.concatenate([late, rest[:, : half - cut]], axis=0)
    kept_upper = jnp.concatenate([kept_upper, rest[:, half - cut :]], axis=0)

    hi, lo, plain_left, sent_left, kept_left = factor(sent_place, block_mask[0], *diag_halves, orders, *panel_halves)

    left_share = lax.dynamic_slice_in_dim(plain_left, col * lower_in.shape[1], lower_in.shape[1], 1)
    share = upper_in.shape[0]
    share_hi = lax.dynamic_slice_in_dim(hi, row * share, share, 0)
    share_lo = lax.dynamic_slice_in_dim(lo, row * share, share, 0)
    left_received = partner(left_share, "cube", 1)
    small, mask = after((row_map[0], block_mask[0].reshape(-1)), hi)
    mask_rows = -(-(2 * rows + mask.shape[0]) // (16 * raw_end)) * 16
    fill = jnp.zeros(mask_rows * raw_end - 2 * rows - mask.shape[0], mask.dtype)
    digits = jnp.concatenate([small // 32, small % 32, mask, fill])
    digits = digits.astype(jnp.bfloat16).reshape(mask_rows, raw_end)

    def choice(order):
        return (order[:, None] == jnp.arange(rows, dtype=jnp.int32)[None, :]).astype(jnp.bfloat16)

    chosen = choice(after(row_map[0], hi))

    bounds = [width * chunk for chunk in range(RAW, CHUNKS + 1)]
    if width % 256 == 0:
        bounds.insert(-1, half - width // 2)
    spans = list(zip(bounds, bounds[1:]))
    sent, received, merged_after = [], [], []
    merged = None

    def merge(number):
        start, end = spans[number]
        return merge_chunk(
            kept_place, hi, lo, kept_left, trailing, chosen, received[number], [kept_upper], [0], start, end - start,
            merged,
        )

    def merge_raw():
        result = merged
        for start in range(0, raw_end, width):
            result = merge_chunk(
                kept_place, hi, lo, kept_left, trailing, chosen, raw_received, [kept_upper], [0], start,
                width, result, (0, other_left, other_right),
            )
        return result

    for number, (start, end) in enumerate(spans):
        before = []
        if number >= AHEAD - 1:
            before += [([raw_received] + received)[number - AHEAD + 1], sent[-1]]
        if number == 1:
            for step in range(1, len(bits_of("row"))):
                late = next_doubled(after(late, sent[0]), "row", 0, step)
        if number == 3:
            before += [left_received]
            for step in range(1, len(bits_of("row"))):
                kept_upper = next_doubled(after(kept_upper, raw_received, sent[2]), "row", 0, step)
            raw_upper = after(early[:, :raw_end], received[0], sent[2])
            right_share = (fast(share_hi, raw_upper) + fast(share_lo, raw_upper)).astype(jnp.bfloat16)
            bundle = partner(jnp.concatenate([right_share, digits], axis=0), "cube", 1)
        if number == 5:
            before += [bundle, kept_upper]
        if number == 6:
            arrived = after(bundle, received[3], sent[5])
            right_received = arrived[:share]
            digits = arrived[share:].reshape(-1).astype(jnp.float32)
            other_order = (32 * digits[:rows] + digits[rows : 2 * rows]).astype(jnp.int32)
            other_flags = digits[2 * rows : 2 * rows + mask.shape[0]].reshape(block_mask.shape[1:])
            other_flags = jnp.where(parity == 0, other_flags[:, :1], other_flags[:, 1:])
            other_chosen = choice(other_order)
            left_received = after(left_received, received[3], sent[5])
            other_left = lax.all_gather(left_received, "col", axis=1, tiled=True)
            other_left = other_left.astype(jnp.float32) * jnp.repeat(other_flags, block_rows, axis=0)
            other_left = other_left.astype(jnp.bfloat16)
        if number == 8:
            other_right = lax.all_gather(after(right_received, received[5], sent[7]), "row", axis=0, tiled=True)
        if number == 9:
            before += [other_left, other_right, other_chosen]
        ready = MERGES.get(number, ())
        for item in ready:
            merged = merge_raw() if item == "raw" else merge(item)
        if ready:
            before += [merged]
        place = after(sent_place, *before) if before else sent_place
        piece, first = (early, 0) if end <= cut else (late, cut)
        sent.append(send_chunk(place, hi, lo, sent_left, trailing, [piece], [first], start, end - start))
        outgoing = sent[-1]
        if number == len(spans) - 1:
            outgoing = fast(other_chosen, outgoing).astype(jnp.bfloat16)
        received.append(partner(outgoing, "cube", 1))

    for number in range(1 + MERGES[max(MERGES)][-1], len(spans) - 1):
        merged = merge(number)
    start, end = spans[-1]
    own = send_chunk(
        after(kept_place, merged), hi, lo, kept_left, trailing, [kept_upper], [0], start, end - start
    )
    merged = join_chunk(own, received[-1], start, merged)
    return merged[None]


def solution(mesh):
    return jax.shard_map(
        local,
        mesh=mesh,
        in_specs=(
            P("cube", ("row", "col"), None),
            P("cube", None),
            P("cube", "row", "col"),
            P("cube", "row", "col"),
            P("cube", "row", "col"),
            P("cube", "row", "col"),
            P("cube", "row"),
        ),
        out_specs=P("cube", "row", "col"),
        check_vma=False,
    )
```

```python
import functools

import jax
import jax.numpy as jnp
from jax import lax
from jax.experimental import pallas as pl
from jax.experimental.pallas import tpu as pltpu
from jax.sharding import PartitionSpec as P

CHUNKS = 15
RAW = 2
EARLY = 2
AHEAD = 3
MERGES = {6: (0,), 7: (1,), 8: (2, 3), 9: (4,), 10: ("raw",), 11: (5, 6), 12: (7, 8)}
ROW_STEPS = 4
HIGH = lax.Precision.HIGHEST
VMEM_LIMIT = 48 * 1024 * 1024


def partner(block, axis, bits):
    count = lax.axis_size(axis)
    return lax.ppermute(block, axis, [(i, i ^ bits) for i in range(count)])


def exact(left, right):
    return jnp.dot(left, right, precision=HIGH, preferred_element_type=jnp.float32)


def fast(left, right):
    return jnp.dot(left, right, preferred_element_type=jnp.float32)


def split(value):
    high = value.astype(jnp.bfloat16)
    return high, (value - high.astype(jnp.float32)).astype(jnp.bfloat16)


def eliminate(block):
    size = block.shape[0]
    row = lax.broadcasted_iota(jnp.int32, (size, size), 0)
    lane = lax.broadcasted_iota(jnp.int32, (size, size), 1)

    def eight(turn, work):
        left = size - 8 * turn
        for step in range(8):
            column = work[:, step : step + 1]
            pivot_row = work[step : step + 1, :]
            inverse = 1.0 / work[step : step + 1, step : step + 1]
            scaled = pivot_row * inverse
            lane_one = lane[:1]
            at = lane_one == step
            passed = (lane_one < step) | (lane_one >= left)
            for_later = jnp.where(at, inverse, scaled)
            for_passed = jnp.where(passed | at, 0.0, scaled)
            row_passed = (row < step) | (row >= left)
            base = jnp.where((lane == step) & jnp.logical_not(row_passed), 0.0, work)
            fresh = base - column * jnp.where(row_passed, for_passed, for_later)
            own = jnp.where(at, inverse, jnp.where(passed, pivot_row, -scaled))
            work = jnp.where(row == step, own, fresh)
        work = jnp.concatenate([work[8:], work[:8]], axis=0)
        return pltpu.roll(work, size - 8, 1)

    return lax.fori_loop(0, size // 8, eight, block)


def inverses(block):
    size = block.shape[0]
    work = eliminate(block)
    row = lax.broadcasted_iota(jnp.int32, (size, size), 0)
    lane = lax.broadcasted_iota(jnp.int32, (size, size), 1)
    diagonal = jnp.sum(jnp.where(row == lane, work, 0.0), axis=0, keepdims=True)
    lower = jnp.where(row > lane, work, jnp.where(row == lane, 1.0, 0.0))
    upper = jnp.where(row < lane, work * diagonal, jnp.where(row == lane, work, 0.0))
    return lower, upper


def factor_kernel(
    place, mask, first, second, orders, left_panel, right_panel, hi, lo, plain, sent, kept
):
    size = first.shape[1]
    half = size // 2
    block = jnp.concatenate([first[...], second[...]], axis=0)
    row = lax.broadcasted_iota(jnp.int32, (size, size), 0)

    def chosen(number):
        return jnp.where(orders[number : number + 1, :] == row, 1.0, 0.0)

    pivoted = exact(chosen(0).T, block)
    lower_one, upper_one = inverses(pivoted[:half, :half])
    lower_side = exact(pivoted[half:, :half], upper_one)
    upper_side = exact(lower_one, pivoted[:half, half:])
    schur = pivoted[half:, half:] - exact(lower_side, upper_side)
    lower_two, upper_two = inverses(schur)
    zero = jnp.zeros((half, half), jnp.float32)
    corner_lower = -exact(lower_two, exact(lower_side, lower_one))
    corner_upper = -exact(upper_one, exact(upper_side, upper_two))
    lower_inv = jnp.concatenate(
        [jnp.concatenate([lower_one, zero], 1), jnp.concatenate([corner_lower, lower_two], 1)], 0
    )
    upper_inv = jnp.concatenate(
        [jnp.concatenate([upper_one, corner_upper], 1), jnp.concatenate([zero, upper_two], 1)], 0
    )
    hi[...], lo[...] = split(exact(lower_inv, chosen(1).T))
    upper_hi, upper_lo = split(exact(chosen(2), upper_inv))
    rows = left_panel.shape[0]
    block_rows = rows // mask.shape[0]
    for start in range(0, rows, size):
        part = jnp.concatenate(
            [left_panel[start : start + size, :], right_panel[start : start + size, :]], axis=1
        )
        result = (fast(part, upper_hi) + fast(part, upper_lo)).astype(jnp.bfloat16)
        plain[start : start + size, :] = result
        result = result.astype(jnp.float32)
        for at in range(start, start + size, block_rows):
            piece = result[at - start : at - start + block_rows]
            number = at // block_rows
            sent[at : at + block_rows, :] = (piece * mask[number, place[0]].astype(jnp.float32)).astype(jnp.bfloat16)
            kept[at : at + block_rows, :] = (piece * mask[number, 1 - place[0]].astype(jnp.float32)).astype(jnp.bfloat16)


def factor(place, mask, first, second, orders, left_panel, right_panel):
    size = first.shape[1]
    rows = left_panel.shape[0]
    half_type = jnp.bfloat16
    scalars = pl.BlockSpec(memory_space=pltpu.SMEM)
    arrays = pl.BlockSpec(memory_space=pltpu.VMEM)
    return pl.pallas_call(
        factor_kernel,
        in_specs=[scalars] * 2 + [arrays] * 5,
        out_shape=(
            jax.ShapeDtypeStruct((size, size), half_type),
            jax.ShapeDtypeStruct((size, size), half_type),
            jax.ShapeDtypeStruct((rows, size), half_type),
            jax.ShapeDtypeStruct((rows, size), half_type),
            jax.ShapeDtypeStruct((rows, size), half_type),
        ),
        compiler_params=pltpu.CompilerParams(vmem_limit_bytes=VMEM_LIMIT),
        cost_estimate=pl.CostEstimate(flops=30_000_000_000, bytes_accessed=3_000_000, transcendentals=0),
        name="factor",
    )(place, mask, first, second, orders, left_panel, right_panel)


def panel_tile(hi, lo, pieces):
    columns = jnp.concatenate([piece[...] for piece in pieces], axis=0)
    return (fast(hi[...], columns) + fast(lo[...], columns)).astype(jnp.bfloat16)


def send_kernel(place, hi, lo, left, trailing, *rest):
    *pieces, out, right = rest

    @pl.when(pl.program_id(0) == 0)
    def _():
        right[...] = panel_tile(hi, lo, pieces)

    out[...] = (trailing[...].astype(jnp.float32) - fast(left[...], right[...])).astype(jnp.bfloat16)


def merge_kernel(place, hi, lo, left, trailing, chosen, received, *rest):
    *pieces, out, right = rest

    @pl.when(pl.program_id(0) == 0)
    def _():
        right[...] = panel_tile(hi, lo, pieces)

    own = (trailing[...].astype(jnp.float32) - fast(left[...], right[...])).astype(jnp.bfloat16)
    out[...] = (own.astype(jnp.float32) + fast(chosen[...], received[...])).astype(jnp.bfloat16)


def merge_kernel_into(place, hi, lo, left, trailing, chosen, received, *rest):
    *pieces, _, out, right = rest
    merge_kernel(place, hi, lo, left, trailing, chosen, received, *pieces, out, right)


def merge_raw_kernel(place, hi, lo, left, trailing, chosen, received, other_left, other_right, *rest):
    *pieces, out, right, updated = rest

    @pl.when(pl.program_id(0) == 0)
    def _():
        size = out.shape[0]
        for first in range(0, received.shape[0], size):
            rows = slice(first, first + size)
            update = fast(other_left[rows, :], other_right[...])
            updated[rows, :] = (received[rows, :].astype(jnp.float32) - update).astype(jnp.bfloat16)

    merge_kernel(place, hi, lo, left, trailing, chosen, updated, *pieces, out, right)


def merge_raw_kernel_into(*refs):
    merge_raw_kernel(*refs[:-4], *refs[-3:])


def specs_for(hi, left, columns, width, start, pieces, starts):
    size = hi.shape[0]
    rows = left.shape[0] // ROW_STEPS
    half_blocks, chunk = columns // 2 // width, start // width
    whole = pl.BlockSpec((size, size), lambda i, place: (0, 0))
    specs = [
        whole,
        whole,
        pl.BlockSpec((rows, size), lambda i, place: (i, 0)),
        pl.BlockSpec((rows, width), lambda i, place: (i, place[0] * half_blocks + chunk)),
    ]
    piece_specs = []
    for piece, first in zip(pieces, starts):
        block = (piece.shape[0], width)
        if first is None:
            piece_specs.append(pl.BlockSpec(block, lambda i, place: (0, place[0] * half_blocks + chunk)))
        else:
            piece_specs.append(pl.BlockSpec(block, lambda i, place, at=(start - first) // width: (0, at)))
    return specs, piece_specs


def send_chunk(place, hi, lo, left, trailing, pieces, starts, start, width):
    rows, columns = trailing.shape
    specs, piece_specs = specs_for(hi, left, columns, width, start, pieces, starts)
    return pl.pallas_call(
        send_kernel,
        grid_spec=pltpu.PrefetchScalarGridSpec(
            num_scalar_prefetch=1,
            grid=(ROW_STEPS,),
            in_specs=specs + piece_specs,
            out_specs=pl.BlockSpec((rows // ROW_STEPS, width), lambda i, place: (i, 0)),
            scratch_shapes=[pltpu.VMEM((hi.shape[0], width), jnp.bfloat16)],
        ),
        out_shape=jax.ShapeDtypeStruct((rows, width), jnp.bfloat16),
        compiler_params=pltpu.CompilerParams(vmem_limit_bytes=VMEM_LIMIT),
        cost_estimate=pl.CostEstimate(flops=2 * rows * 256 * width, bytes_accessed=5 * rows * width, transcendentals=0),
        name="send_part",
    )(place, hi, lo, left, trailing, *pieces)


def merge_chunk(place, hi, lo, left, trailing, chosen, received, pieces, starts, start, width, merged, raw=None):
    rows, columns = trailing.shape
    step_rows = rows // ROW_STEPS
    specs, piece_specs = specs_for(hi, left, columns, width, start, pieces, starts)
    specs.append(pl.BlockSpec((step_rows, rows), lambda i, place: (i, 0)))
    operands = [place, hi, lo, left, trailing, chosen, received]
    scratch = [pltpu.VMEM((hi.shape[0], width), jnp.bfloat16)]
    body, body_into = merge_kernel, merge_kernel_into
    if raw is None:
        specs.append(pl.BlockSpec((rows, width), lambda i, place: (0, 0)))
    else:
        first, other_left, other_right = raw
        at = (start - first) // width
        specs.append(pl.BlockSpec((rows, width), lambda i, place: (0, at)))
        specs.append(pl.BlockSpec(other_left.shape, lambda i, place: (0, 0)))
        specs.append(pl.BlockSpec((other_right.shape[0], width), lambda i, place: (0, at)))
        operands += [other_left, other_right]
        scratch.append(pltpu.VMEM((rows, width), jnp.bfloat16))
        body, body_into = merge_raw_kernel, merge_raw_kernel_into
    specs += piece_specs
    operands += pieces
    aliases = {}
    if merged is not None:
        aliases = {len(operands): 0}
        operands.append(merged)
        specs.append(pl.BlockSpec(memory_space=pl.ANY))
        body = body_into
    chunk = start // width
    return pl.pallas_call(
        body,
        grid_spec=pltpu.PrefetchScalarGridSpec(
            num_scalar_prefetch=1,
            grid=(ROW_STEPS,),
            in_specs=specs,
            out_specs=pl.BlockSpec((step_rows, width), lambda i, place: (i, chunk)),
            scratch_shapes=scratch,
        ),
        out_shape=jax.ShapeDtypeStruct((rows, columns // 2), jnp.bfloat16),
        input_output_aliases=aliases,
        compiler_params=pltpu.CompilerParams(vmem_limit_bytes=VMEM_LIMIT),
        cost_estimate=pl.CostEstimate(flops=2 * rows * (rows + 256) * width, bytes_accessed=8 * rows * width, transcendentals=0),
        name="merge_part",
    )(*operands)


def join_kernel(own, received, _, out):
    out[...] = (own[...].astype(jnp.float32) + received[...].astype(jnp.float32)).astype(jnp.bfloat16)


def join_chunk(own, received, start, merged):
    rows, width = own.shape
    step_rows = rows // 2
    part = pl.BlockSpec((step_rows, width), lambda i: (i, 0))
    return pl.pallas_call(
        join_kernel,
        grid=(2,),
        in_specs=[part, part, pl.BlockSpec(memory_space=pl.ANY)],
        out_specs=pl.BlockSpec((step_rows, width), lambda i: (i, start // width)),
        out_shape=jax.ShapeDtypeStruct(merged.shape, merged.dtype),
        input_output_aliases={2: 0},
        compiler_params=pltpu.CompilerParams(vmem_limit_bytes=VMEM_LIMIT),
        cost_estimate=pl.CostEstimate(flops=rows * width, bytes_accessed=6 * rows * width, transcendentals=0),
        name="join_part",
    )(own, received, merged)


def bits_of(axis):
    bits = [1 << bit for bit in reversed(range((lax.axis_size(axis) - 1).bit_length()))]
    if not isinstance(axis, str):
        last = lax.axis_size(axis[1:])
        bits = [bit for bit in bits if bit != last] + [last]
    return bits


def doubled(block, axis, dimension):
    for step in range(len(bits_of(axis))):
        block = next_doubled(block, axis, dimension, step)
    return block


def halves(block, axis, dimension):
    steps = len(bits_of(axis))
    for step in range(steps - 1):
        block = next_doubled(block, axis, dimension, step)
    return block, partner(block, axis, bits_of(axis)[steps - 1])


def next_doubled(block, axis, dimension, step):
    return jnp.concatenate([block, partner(block, axis, bits_of(axis)[step])], axis=dimension)


def place_of(index, part, axis):
    apart = (index // part) ^ lax.axis_index(axis)
    place = jnp.zeros_like(index)
    for number, bits in enumerate(bits_of(axis)):
        place = place + jnp.where(apart & bits != 0, 1 << number, 0)
    return place * part + index % part


def after(value, *others):
    return lax.optimization_barrier((value, *others))[0]


def local(diag_block, pivot_order, lower_in, upper_in, trailing, block_mask, row_map):
    diag_block, lower_in, upper_in, trailing = diag_block[0], lower_in[0], upper_in[0], trailing[0]
    size = diag_block.shape[1]
    rows, columns = trailing.shape
    half = columns // 2
    width = half // CHUNKS
    row, col = lax.axis_index("row"), lax.axis_index("col")
    parity = lax.axis_index("cube") % 2
    sent_place = (1 - parity).astype(jnp.int32).reshape(1)
    kept_place = parity.astype(jnp.int32).reshape(1)
    raw_rest = width // 4 if width % 512 == 0 else 0
    raw_end = RAW * width + raw_rest

    raw = lax.dynamic_slice_in_dim(trailing, (1 - parity) * half, raw_end, 1)
    raw_received = partner(raw, "cube", 1)

    diag_halves = halves(after(diag_block, raw), ("row", "col"), 0)
    panel_halves = halves(lower_in, "col", 1)
    order = pivot_order[0]
    every = jnp.arange(size, dtype=jnp.int32)
    orders = jnp.stack([
        place_of(order, diag_block.shape[0], ("row", "col")),
        place_of(order, upper_in.shape[0], "row"),
        place_of(every, lower_in.shape[1], "col"),
    ])
    block_rows = rows // block_mask.shape[1]

    def columns_of(place, first, last):
        return lax.dynamic_slice_in_dim(upper_in, place * half + first, last - first, 1)

    cut = (RAW + EARLY) * width
    early = doubled(columns_of(1 - parity, 0, cut), "row", 0)
    late, kept_upper = columns_of(1 - parity, cut, half), columns_of(parity, 0, half)
    rest = partner(jnp.concatenate([late, kept_upper], axis=1), "row", bits_of("row")[0])
    late = jnp.concatenate([late, rest[:, : half - cut]], axis=0)
    kept_upper = jnp.concatenate([kept_upper, rest[:, half - cut :]], axis=0)

    hi, lo, plain_left, sent_left, kept_left = factor(sent_place, block_mask[0], *diag_halves, orders, *panel_halves)

    left_share = lax.dynamic_slice_in_dim(plain_left, col * lower_in.shape[1], lower_in.shape[1], 1)
    share = upper_in.shape[0]
    share_hi = lax.dynamic_slice_in_dim(hi, row * share, share, 0)
    share_lo = lax.dynamic_slice_in_dim(lo, row * share, share, 0)
    left_received = partner(left_share, "cube", 1)
    small, mask = after((row_map[0], block_mask[0].reshape(-1)), hi)
    mask_rows = -(-(2 * rows + mask.shape[0]) // (16 * raw_end)) * 16
    fill = jnp.zeros(mask_rows * raw_end - 2 * rows - mask.shape[0], mask.dtype)
    digits = jnp.concatenate([small // 32, small % 32, mask, fill])
    digits = digits.astype(jnp.bfloat16).reshape(mask_rows, raw_end)

    def choice(order):
        return (order[:, None] == jnp.arange(rows, dtype=jnp.int32)[None, :]).astype(jnp.bfloat16)

    chosen = choice(after(row_map[0], hi))

    bounds = [width * chunk for chunk in range(RAW, CHUNKS + 1)]
    if width % 256 == 0:
        bounds.insert(-1, half - width // 2)
    bounds[0] = raw_end
    spans = list(zip(bounds, bounds[1:]))
    sent, received, merged_after = [], [], []
    merged = None

    def merge(number):
        start, end = spans[number]
        return merge_chunk(
            kept_place, hi, lo, kept_left, trailing, chosen, received[number], [kept_upper], [0], start, end - start,
            merged,
        )

    def merge_raw():
        result = merged
        tiles = [(start, width) for start in range(0, raw_end - raw_rest, width)]
        if raw_rest:
            tiles.append((raw_end - raw_rest, raw_rest))
        for start, tile in tiles:
            result = merge_chunk(
                kept_place, hi, lo, kept_left, trailing, chosen, raw_received, [kept_upper], [0], start, tile, result,
                (0, other_left, other_right),
            )
        return result

    for number, (start, end) in enumerate(spans):
        before = []
        if number >= AHEAD - 1:
            before += [([raw_received] + received)[number - AHEAD + 1], sent[-1]]
        if number == 1:
            for step in range(1, len(bits_of("row"))):
                late = next_doubled(after(late, sent[0]), "row", 0, step)
        if number == 3:
            before += [left_received]
            for step in range(1, len(bits_of("row"))):
                kept_upper = next_doubled(after(kept_upper, raw_received, sent[2]), "row", 0, step)
            raw_upper = after(early[:, :raw_end], received[0], sent[2])
            right_share = (fast(share_hi, raw_upper) + fast(share_lo, raw_upper)).astype(jnp.bfloat16)
            bundle = partner(jnp.concatenate([right_share, digits], axis=0), "cube", 1)
        if number == 5:
            before += [bundle, kept_upper]
        if number == 6:
            arrived = after(bundle, received[3], sent[5])
            right_received = arrived[:share]
            digits = arrived[share:].reshape(-1).astype(jnp.float32)
            other_order = (32 * digits[:rows] + digits[rows : 2 * rows]).astype(jnp.int32)
            other_flags = digits[2 * rows : 2 * rows + mask.shape[0]].reshape(block_mask.shape[1:])
            other_flags = jnp.where(parity == 0, other_flags[:, :1], other_flags[:, 1:])
            other_chosen = choice(other_order)
            left_received = after(left_received, received[3], sent[5])
            other_left = lax.all_gather(left_received, "col", axis=1, tiled=True)
            other_left = other_left.astype(jnp.float32) * jnp.repeat(other_flags, block_rows, axis=0)
            other_left = other_left.astype(jnp.bfloat16)
        if number == 8:
            other_right = lax.all_gather(after(right_received, received[5], sent[7]), "row", axis=0, tiled=True)
        if number == 9:
            before += [other_left, other_right, other_chosen]
        ready = MERGES.get(number, ())
        for item in ready:
            merged = merge_raw() if item == "raw" else merge(item)
        if ready:
            before += [merged]
        place = after(sent_place, *before) if before else sent_place
        piece, first = (early, 0) if end <= cut else (late, cut)
        sent.append(send_chunk(place, hi, lo, sent_left, trailing, [piece], [first], start, end - start))
        outgoing = sent[-1]
        if number == len(spans) - 1:
            outgoing = fast(other_chosen, outgoing).astype(jnp.bfloat16)
        received.append(partner(outgoing, "cube", 1))

    for number in range(1 + MERGES[max(MERGES)][-1], len(spans) - 1):
        merged = merge(number)
    start, end = spans[-1]
    own = send_chunk(
        after(kept_place, merged), hi, lo, kept_left, trailing, [kept_upper], [0], start, end - start
    )
    merged = join_chunk(own, received[-1], start, merged)
    return merged[None]


def solution(mesh):
    return jax.shard_map(
        local,
        mesh=mesh,
        in_specs=(
            P("cube", ("row", "col"), None),
            P("cube", None),
            P("cube", "row", "col"),
            P("cube", "row", "col"),
            P("cube", "row", "col"),
            P("cube", "row", "col"),
            P("cube", "row"),
        ),
        out_specs=P("cube", "row", "col"),
        check_vma=False,
    )
```

```python
import functools

import jax
import jax.numpy as jnp
from jax import lax
from jax.experimental import pallas as pl
from jax.experimental.pallas import tpu as pltpu
from jax.sharding import PartitionSpec as P

CHUNKS = 15
RAW = 2
EARLY = 2
LATE_CUT = 6
KEPT_CUTS = (0, 4, 8, 12, 15)
AHEAD = 3
MERGES = {6: (0,), 7: (1,), 8: (2, 3), 9: (4,), 10: ("raw",), 11: (5, 6), 12: (7, 8)}
ROW_STEPS = 4
HIGH = lax.Precision.HIGHEST
VMEM_LIMIT = 48 * 1024 * 1024


def partner(block, axis, bits):
    count = lax.axis_size(axis)
    return lax.ppermute(block, axis, [(i, i ^ bits) for i in range(count)])


def exact(left, right):
    return jnp.dot(left, right, precision=HIGH, preferred_element_type=jnp.float32)


def fast(left, right):
    return jnp.dot(left, right, preferred_element_type=jnp.float32)


def split(value):
    high = value.astype(jnp.bfloat16)
    return high, (value - high.astype(jnp.float32)).astype(jnp.bfloat16)


def eliminate(block):
    size = block.shape[0]
    row = lax.broadcasted_iota(jnp.int32, (size, size), 0)
    lane = lax.broadcasted_iota(jnp.int32, (size, size), 1)

    def eight(turn, work):
        left = size - 8 * turn
        for step in range(8):
            column = work[:, step : step + 1]
            pivot_row = work[step : step + 1, :]
            inverse = 1.0 / work[step : step + 1, step : step + 1]
            scaled = pivot_row * inverse
            lane_one = lane[:1]
            at = lane_one == step
            passed = (lane_one < step) | (lane_one >= left)
            for_later = jnp.where(at, inverse, scaled)
            for_passed = jnp.where(passed | at, 0.0, scaled)
            row_passed = (row < step) | (row >= left)
            base = jnp.where((lane == step) & jnp.logical_not(row_passed), 0.0, work)
            fresh = base - column * jnp.where(row_passed, for_passed, for_later)
            own = jnp.where(at, inverse, jnp.where(passed, pivot_row, -scaled))
            work = jnp.where(row == step, own, fresh)
        work = jnp.concatenate([work[8:], work[:8]], axis=0)
        return pltpu.roll(work, size - 8, 1)

    return lax.fori_loop(0, size // 8, eight, block)


def inverses(block):
    size = block.shape[0]
    work = eliminate(block)
    row = lax.broadcasted_iota(jnp.int32, (size, size), 0)
    lane = lax.broadcasted_iota(jnp.int32, (size, size), 1)
    diagonal = jnp.sum(jnp.where(row == lane, work, 0.0), axis=0, keepdims=True)
    lower = jnp.where(row > lane, work, jnp.where(row == lane, 1.0, 0.0))
    upper = jnp.where(row < lane, work * diagonal, jnp.where(row == lane, work, 0.0))
    return lower, upper


def factor_kernel(
    place, mask, first, second, orders, left_panel, right_panel, hi, lo, plain, sent, kept
):
    size = first.shape[1]
    half = size // 2
    block = jnp.concatenate([first[...], second[...]], axis=0)
    row = lax.broadcasted_iota(jnp.int32, (size, size), 0)

    def chosen(number):
        return jnp.where(orders[number : number + 1, :] == row, 1.0, 0.0)

    pivoted = exact(chosen(0).T, block)
    lower_one, upper_one = inverses(pivoted[:half, :half])
    lower_side = exact(pivoted[half:, :half], upper_one)
    upper_side = exact(lower_one, pivoted[:half, half:])
    schur = pivoted[half:, half:] - exact(lower_side, upper_side)
    lower_two, upper_two = inverses(schur)
    zero = jnp.zeros((half, half), jnp.float32)
    corner_lower = -exact(lower_two, exact(lower_side, lower_one))
    corner_upper = -exact(upper_one, exact(upper_side, upper_two))
    lower_inv = jnp.concatenate(
        [jnp.concatenate([lower_one, zero], 1), jnp.concatenate([corner_lower, lower_two], 1)], 0
    )
    upper_inv = jnp.concatenate(
        [jnp.concatenate([upper_one, corner_upper], 1), jnp.concatenate([zero, upper_two], 1)], 0
    )
    hi[...], lo[...] = split(exact(lower_inv, chosen(1).T))
    upper_hi, upper_lo = split(exact(chosen(2), upper_inv))
    rows = left_panel.shape[0]
    block_rows = rows // mask.shape[0]
    for start in range(0, rows, size):
        part = jnp.concatenate(
            [left_panel[start : start + size, :], right_panel[start : start + size, :]], axis=1
        )
        result = (fast(part, upper_hi) + fast(part, upper_lo)).astype(jnp.bfloat16)
        plain[start : start + size, :] = result
        result = result.astype(jnp.float32)
        for at in range(start, start + size, block_rows):
            piece = result[at - start : at - start + block_rows]
            number = at // block_rows
            sent[at : at + block_rows, :] = (piece * mask[number, place[0]].astype(jnp.float32)).astype(jnp.bfloat16)
            kept[at : at + block_rows, :] = (piece * mask[number, 1 - place[0]].astype(jnp.float32)).astype(jnp.bfloat16)


def factor(place, mask, first, second, orders, left_panel, right_panel):
    size = first.shape[1]
    rows = left_panel.shape[0]
    half_type = jnp.bfloat16
    scalars = pl.BlockSpec(memory_space=pltpu.SMEM)
    arrays = pl.BlockSpec(memory_space=pltpu.VMEM)
    return pl.pallas_call(
        factor_kernel,
        in_specs=[scalars] * 2 + [arrays] * 5,
        out_shape=(
            jax.ShapeDtypeStruct((size, size), half_type),
            jax.ShapeDtypeStruct((size, size), half_type),
            jax.ShapeDtypeStruct((rows, size), half_type),
            jax.ShapeDtypeStruct((rows, size), half_type),
            jax.ShapeDtypeStruct((rows, size), half_type),
        ),
        compiler_params=pltpu.CompilerParams(vmem_limit_bytes=VMEM_LIMIT),
        cost_estimate=pl.CostEstimate(flops=30_000_000_000, bytes_accessed=3_000_000, transcendentals=0),
        name="factor",
    )(place, mask, first, second, orders, left_panel, right_panel)


def panel_tile(hi, lo, pieces):
    columns = jnp.concatenate([piece[...] for piece in pieces], axis=0)
    return (fast(hi[...], columns) + fast(lo[...], columns)).astype(jnp.bfloat16)


def send_kernel(place, hi, lo, left, trailing, *rest):
    *pieces, out, right = rest

    @pl.when(pl.program_id(0) == 0)
    def _():
        right[...] = panel_tile(hi, lo, pieces)

    out[...] = (trailing[...].astype(jnp.float32) - fast(left[...], right[...])).astype(jnp.bfloat16)


def merge_kernel(place, hi, lo, left, trailing, chosen, received, *rest):
    *pieces, out, right = rest

    @pl.when(pl.program_id(0) == 0)
    def _():
        right[...] = panel_tile(hi, lo, pieces)

    own = (trailing[...].astype(jnp.float32) - fast(left[...], right[...])).astype(jnp.bfloat16)
    out[...] = (own.astype(jnp.float32) + fast(chosen[...], received[...])).astype(jnp.bfloat16)


def merge_kernel_into(place, hi, lo, left, trailing, chosen, received, *rest):
    *pieces, _, out, right = rest
    merge_kernel(place, hi, lo, left, trailing, chosen, received, *pieces, out, right)


def merge_raw_kernel(place, hi, lo, left, trailing, chosen, received, other_left, other_right, *rest):
    *pieces, out, right, updated = rest

    @pl.when(pl.program_id(0) == 0)
    def _():
        size = out.shape[0]
        for first in range(0, received.shape[0], size):
            rows = slice(first, first + size)
            update = fast(other_left[rows, :], other_right[...])
            updated[rows, :] = (received[rows, :].astype(jnp.float32) - update).astype(jnp.bfloat16)

    merge_kernel(place, hi, lo, left, trailing, chosen, updated, *pieces, out, right)


def merge_raw_kernel_into(*refs):
    merge_raw_kernel(*refs[:-4], *refs[-3:])


def specs_for(hi, left, columns, width, start, pieces, starts):
    size = hi.shape[0]
    rows = left.shape[0] // ROW_STEPS
    half_blocks, chunk = columns // 2 // width, start // width
    whole = pl.BlockSpec((size, size), lambda i, place: (0, 0))
    specs = [
        whole,
        whole,
        pl.BlockSpec((rows, size), lambda i, place: (i, 0)),
        pl.BlockSpec((rows, width), lambda i, place: (i, place[0] * half_blocks + chunk)),
    ]
    piece_specs = []
    for piece, first in zip(pieces, starts):
        block = (piece.shape[0], width)
        if first is None:
            piece_specs.append(pl.BlockSpec(block, lambda i, place: (0, place[0] * half_blocks + chunk)))
        else:
            piece_specs.append(pl.BlockSpec(block, lambda i, place, at=(start - first) // width: (0, at)))
    return specs, piece_specs


def send_chunk(place, hi, lo, left, trailing, pieces, starts, start, width):
    rows, columns = trailing.shape
    specs, piece_specs = specs_for(hi, left, columns, width, start, pieces, starts)
    return pl.pallas_call(
        send_kernel,
        grid_spec=pltpu.PrefetchScalarGridSpec(
            num_scalar_prefetch=1,
            grid=(ROW_STEPS,),
            in_specs=specs + piece_specs,
            out_specs=pl.BlockSpec((rows // ROW_STEPS, width), lambda i, place: (i, 0)),
            scratch_shapes=[pltpu.VMEM((hi.shape[0], width), jnp.bfloat16)],
        ),
        out_shape=jax.ShapeDtypeStruct((rows, width), jnp.bfloat16),
        compiler_params=pltpu.CompilerParams(vmem_limit_bytes=VMEM_LIMIT),
        cost_estimate=pl.CostEstimate(flops=2 * rows * 256 * width, bytes_accessed=5 * rows * width, transcendentals=0),
        name="send_part",
    )(place, hi, lo, left, trailing, *pieces)


def merge_chunk(place, hi, lo, left, trailing, chosen, received, pieces, starts, start, width, merged, raw=None):
    rows, columns = trailing.shape
    step_rows = rows // ROW_STEPS
    specs, piece_specs = specs_for(hi, left, columns, width, start, pieces, starts)
    specs.append(pl.BlockSpec((step_rows, rows), lambda i, place: (i, 0)))
    operands = [place, hi, lo, left, trailing, chosen, received]
    scratch = [pltpu.VMEM((hi.shape[0], width), jnp.bfloat16)]
    body, body_into = merge_kernel, merge_kernel_into
    if raw is None:
        specs.append(pl.BlockSpec((rows, width), lambda i, place: (0, 0)))
    else:
        first, other_left, other_right = raw
        at = (start - first) // width
        specs.append(pl.BlockSpec((rows, width), lambda i, place: (0, at)))
        specs.append(pl.BlockSpec(other_left.shape, lambda i, place: (0, 0)))
        specs.append(pl.BlockSpec((other_right.shape[0], width), lambda i, place: (0, at)))
        operands += [other_left, other_right]
        scratch.append(pltpu.VMEM((rows, width), jnp.bfloat16))
        body, body_into = merge_raw_kernel, merge_raw_kernel_into
    specs += piece_specs
    operands += pieces
    aliases = {}
    if merged is not None:
        aliases = {len(operands): 0}
        operands.append(merged)
        specs.append(pl.BlockSpec(memory_space=pl.ANY))
        body = body_into
    chunk = start // width
    return pl.pallas_call(
        body,
        grid_spec=pltpu.PrefetchScalarGridSpec(
            num_scalar_prefetch=1,
            grid=(ROW_STEPS,),
            in_specs=specs,
            out_specs=pl.BlockSpec((step_rows, width), lambda i, place: (i, chunk)),
            scratch_shapes=scratch,
        ),
        out_shape=jax.ShapeDtypeStruct((rows, columns // 2), jnp.bfloat16),
        input_output_aliases=aliases,
        compiler_params=pltpu.CompilerParams(vmem_limit_bytes=VMEM_LIMIT),
        cost_estimate=pl.CostEstimate(flops=2 * rows * (rows + 256) * width, bytes_accessed=8 * rows * width, transcendentals=0),
        name="merge_part",
    )(*operands)


def join_kernel(own, received, _, out):
    out[...] = (own[...].astype(jnp.float32) + received[...].astype(jnp.float32)).astype(jnp.bfloat16)


def join_chunk(own, received, start, merged):
    rows, width = own.shape
    step_rows = rows // 2
    part = pl.BlockSpec((step_rows, width), lambda i: (i, 0))
    return pl.pallas_call(
        join_kernel,
        grid=(2,),
        in_specs=[part, part, pl.BlockSpec(memory_space=pl.ANY)],
        out_specs=pl.BlockSpec((step_rows, width), lambda i: (i, start // width)),
        out_shape=jax.ShapeDtypeStruct(merged.shape, merged.dtype),
        input_output_aliases={2: 0},
        compiler_params=pltpu.CompilerParams(vmem_limit_bytes=VMEM_LIMIT),
        cost_estimate=pl.CostEstimate(flops=rows * width, bytes_accessed=6 * rows * width, transcendentals=0),
        name="join_part",
    )(own, received, merged)


def bits_of(axis):
    bits = [1 << bit for bit in reversed(range((lax.axis_size(axis) - 1).bit_length()))]
    if not isinstance(axis, str):
        last = lax.axis_size(axis[1:])
        bits = [bit for bit in bits if bit != last] + [last]
    return bits


def doubled(block, axis, dimension):
    for step in range(len(bits_of(axis))):
        block = next_doubled(block, axis, dimension, step)
    return block


def halves(block, axis, dimension):
    steps = len(bits_of(axis))
    for step in range(steps - 1):
        block = next_doubled(block, axis, dimension, step)
    return block, partner(block, axis, bits_of(axis)[steps - 1])


def next_doubled(block, axis, dimension, step):
    return jnp.concatenate([block, partner(block, axis, bits_of(axis)[step])], axis=dimension)


def place_of(index, part, axis):
    apart = (index // part) ^ lax.axis_index(axis)
    place = jnp.zeros_like(index)
    for number, bits in enumerate(bits_of(axis)):
        place = place + jnp.where(apart & bits != 0, 1 << number, 0)
    return place * part + index % part


def after(value, *others):
    return lax.optimization_barrier((value, *others))[0]


def local(diag_block, pivot_order, lower_in, upper_in, trailing, block_mask, row_map):
    diag_block, lower_in, upper_in, trailing = diag_block[0], lower_in[0], upper_in[0], trailing[0]
    size = diag_block.shape[1]
    rows, columns = trailing.shape
    half = columns // 2
    width = half // CHUNKS
    row, col = lax.axis_index("row"), lax.axis_index("col")
    parity = lax.axis_index("cube") % 2
    sent_place = (1 - parity).astype(jnp.int32).reshape(1)
    kept_place = parity.astype(jnp.int32).reshape(1)
    raw_rest = width // 4 if width % 512 == 0 else 0
    raw_end = RAW * width + raw_rest

    raw = lax.dynamic_slice_in_dim(trailing, (1 - parity) * half, raw_end, 1)
    raw_received = partner(raw, "cube", 1)

    diag_halves = halves(after(diag_block, raw), ("row", "col"), 0)
    panel_halves = halves(lower_in, "col", 1)
    order = pivot_order[0]
    every = jnp.arange(size, dtype=jnp.int32)
    orders = jnp.stack([
        place_of(order, diag_block.shape[0], ("row", "col")),
        place_of(order, upper_in.shape[0], "row"),
        place_of(every, lower_in.shape[1], "col"),
    ])
    block_rows = rows // block_mask.shape[1]

    def columns_of(place, first, last):
        return lax.dynamic_slice_in_dim(upper_in, place * half + first, last - first, 1)

    cut = (RAW + EARLY) * width
    early = doubled(columns_of(1 - parity, 0, cut), "row", 0)
    late, kept_upper = columns_of(1 - parity, cut, half), columns_of(parity, 0, half)
    rest = partner(jnp.concatenate([late, kept_upper], axis=1), "row", bits_of("row")[0])
    late = jnp.concatenate([late, rest[:, : half - cut]], axis=0)
    kept_upper = jnp.concatenate([kept_upper, rest[:, half - cut :]], axis=0)

    hi, lo, plain_left, sent_left, kept_left = factor(sent_place, block_mask[0], *diag_halves, orders, *panel_halves)

    left_share = lax.dynamic_slice_in_dim(plain_left, col * lower_in.shape[1], lower_in.shape[1], 1)
    share = upper_in.shape[0]
    share_hi = lax.dynamic_slice_in_dim(hi, row * share, share, 0)
    share_lo = lax.dynamic_slice_in_dim(lo, row * share, share, 0)
    left_received = partner(left_share, "cube", 1)
    small, mask = after((row_map[0], block_mask[0].reshape(-1)), hi)
    mask_rows = -(-(2 * rows + mask.shape[0]) // (16 * raw_end)) * 16
    fill = jnp.zeros(mask_rows * raw_end - 2 * rows - mask.shape[0], mask.dtype)
    digits = jnp.concatenate([small // 32, small % 32, mask, fill])
    digits = digits.astype(jnp.bfloat16).reshape(mask_rows, raw_end)

    def choice(order):
        return (order[:, None] == jnp.arange(rows, dtype=jnp.int32)[None, :]).astype(jnp.bfloat16)

    chosen = choice(after(row_map[0], hi))

    bounds = [width * chunk for chunk in range(RAW, CHUNKS + 1)]
    if width % 256 == 0:
        bounds.insert(-1, half - width // 2)
    bounds[0] = raw_end
    spans = list(zip(bounds, bounds[1:]))
    sent, received, kept_parts = [], [], []

    def finished(block, first, last, *before):
        block = after(block[:, first:last], *before)
        for step in range(1, len(bits_of("row"))):
            block = next_doubled(block, "row", 0, step)
        return block

    def kept_at(start):
        number = max(n for n in range(4) if KEPT_CUTS[n] * width <= start)
        return [kept_parts[number]], [KEPT_CUTS[number] * width]

    merged = None

    def merge(number):
        start, end = spans[number]
        return merge_chunk(
            kept_place, hi, lo, kept_left, trailing, chosen, received[number], *kept_at(start), start, end - start,
            merged,
        )

    def merge_raw():
        result = merged
        tiles = [(start, width) for start in range(0, raw_end - raw_rest, width)]
        if raw_rest:
            tiles.append((raw_end - raw_rest, raw_rest))
        for start, tile in tiles:
            result = merge_chunk(
                kept_place, hi, lo, kept_left, trailing, chosen, raw_received, *kept_at(start), start, tile, result,
                (0, other_left, other_right),
            )
        return result

    for number, (start, end) in enumerate(spans):
        before = []
        if number >= AHEAD - 1:
            before += [([raw_received] + received)[number - AHEAD + 1], sent[-1]]
        if number == 1:
            late = [finished(late, 0, LATE_CUT * width - cut, sent[0]), late]
        if number == 3:
            late[1] = finished(late[1], LATE_CUT * width - cut, half - cut, raw_received, sent[2])
        if 4 <= number < 8:
            first, last = KEPT_CUTS[number - 4] * width, KEPT_CUTS[number - 3] * width
            kept_parts.append(finished(kept_upper, first, last, received[number - 4], sent[-1]))
        if 6 <= number < 10:
            before += [kept_parts[number - 6]]
        if number == 3:
            before += [left_received]
            raw_upper = after(early[:, :raw_end], received[0], sent[2])
            right_share = (fast(share_hi, raw_upper) + fast(share_lo, raw_upper)).astype(jnp.bfloat16)
            bundle = partner(jnp.concatenate([right_share, digits], axis=0), "cube", 1)
        if number == 5:
            before += [bundle]
        if number == 7:
            arrived = after(bundle, received[4], sent[6])
            right_received = arrived[:share]
            digits = arrived[share:].reshape(-1).astype(jnp.float32)
            other_order = (32 * digits[:rows] + digits[rows : 2 * rows]).astype(jnp.int32)
            other_flags = digits[2 * rows : 2 * rows + mask.shape[0]].reshape(block_mask.shape[1:])
            other_flags = jnp.where(parity == 0, other_flags[:, :1], other_flags[:, 1:])
            other_chosen = choice(other_order)
            left_received = after(left_received, received[4], sent[6])
            other_left = lax.all_gather(left_received, "col", axis=1, tiled=True)
            other_left = other_left.astype(jnp.float32) * jnp.repeat(other_flags, block_rows, axis=0)
            other_left = other_left.astype(jnp.bfloat16)
        if number == 8:
            other_right = lax.all_gather(after(right_received, received[5], sent[7]), "row", axis=0, tiled=True)
        if number == 9:
            before += [other_left, other_right, other_chosen]
        ready = MERGES.get(number, ())
        for item in ready:
            merged = merge_raw() if item == "raw" else merge(item)
        if ready:
            before += [merged]
        place = after(sent_place, *before) if before else sent_place
        if end <= cut:
            piece, first = early, 0
        elif end <= LATE_CUT * width:
            piece, first = late[0], cut
        else:
            piece, first = late[1], LATE_CUT * width
        sent.append(send_chunk(place, hi, lo, sent_left, trailing, [piece], [first], start, end - start))
        outgoing = sent[-1]
        if number == len(spans) - 1:
            outgoing = fast(other_chosen, outgoing).astype(jnp.bfloat16)
        received.append(partner(outgoing, "cube", 1))

    for number in range(1 + MERGES[max(MERGES)][-1], len(spans) - 1):
        merged = merge(number)
    start, end = spans[-1]
    own = send_chunk(
        after(kept_place, merged), hi, lo, kept_left, trailing, *kept_at(start), start, end - start
    )
    merged = join_chunk(own, received[-1], start, merged)
    return merged[None]


def solution(mesh):
    return jax.shard_map(
        local,
        mesh=mesh,
        in_specs=(
            P("cube", ("row", "col"), None),
            P("cube", None),
            P("cube", "row", "col"),
            P("cube", "row", "col"),
            P("cube", "row", "col"),
            P("cube", "row", "col"),
            P("cube", "row"),
        ),
        out_specs=P("cube", "row", "col"),
        check_vma=False,
    )
```
